32 devices in a mesh: section: 2 (over core), dp: 4 (over z), tensor: 4 (over y, x).
Axes of the slice: x: 2, y: 2, z: 4, core: 2. Of those that a mesh axis runs over, the one named last changes fastest.
Arguments:
- layer_in: bfloat16 [2, 4, 2048, 1024], P('section', None, ('dp', 'tensor')), may hold values from -6 to 6
- segments: int32 [2, 4, 4, 512], P(None, None, 'dp'), may hold values from 0 to 3, never falling along the last dimension, each value on 1 to 256 neighbouring positions
- cotangent: bfloat16 [4, 2048, 1024], P(None, ('dp', 'tensor')), may hold values from -6 to 6
- self_qkv: bfloat16 [2, 1024, 3072], P('section', None, 'tensor'), may hold values from -0.1875 to 0.1875
- self_out: bfloat16 [2, 1024, 1024], P('section', 'tensor'), may hold values from -0.75 to 0.75
- cross_proj: bfloat16 [2, 1024, 2048], P('section', None, 'tensor'), may hold values from -0.75 to 0.75
- ffn_up: bfloat16 [2, 1024, 4096], P('section', None, 'tensor'), may hold values from -0.1875 to 0.1875
- ffn_down: bfloat16 [2, 4096, 1024], P('section', 'tensor'), may hold values from -0.09375 to 0.09375
- norm_gain: float32 [2, 3, 1024], P('section'), may hold values from 0.1 to 1.9
- norm_bias: float32 [2, 3, 1024], P('section'), may hold values from -1.8 to 1.8
Outputs:
- layer_out: bfloat16 [2, 4, 2048, 1024], P('section', None, ('dp', 'tensor'))
- input_grad: bfloat16 [2, 4, 2048, 1024], P('section', None, ('dp', 'tensor'))
- self_qkv_grad: float32 [2, 1024, 3072], P('section', None, 'tensor')
- self_out_grad: float32 [2, 1024, 1024], P('section', 'tensor')
- cross_grad: float32 [2, 1024, 2048], P('section', None, 'tensor')
- ffn_up_grad: float32 [2, 1024, 4096], P('section', None, 'tensor')
- ffn_down_grad: float32 [2, 4096, 1024], P('section', 'tensor')
- gain_grad: float32 [2, 3, 1024], P('section', None, 'tensor')
- bias_grad: float32 [2, 3, 1024], P('section', None, 'tensor')
The draws below stay inside these ranges and needn't reach their ends.
Inputs may be any that keep to these rules, and one draw needn't show every extreme that they name: `segments`: every packed row of 512 tokens holds documents 0 to 3 in order, each of 1 to 256 tokens, so every decoder document has its namesake in the encoder row of the same place.
All inputs are finite; a program needn't handle non-finite values.
Results may differ from the reference program's by a relative error of at most 0.03.
Values may be sent and summed in bfloat16 or wider, within the bound.
No kernel may reach another device: no remote copies, remote signals or barrier semaphores. Data moves between devices by JAX's collectives and lax.ppermute only.
A program may use at most 320 MiB of HBM per device.

```python
import math
from functools import partial
import jax
import jax.numpy as jnp
import numpy as np
from jax import lax

D = 1024
HEADS = 16
HD = 64
FF = 4096
LEN = 512
SEGS = 4
SEG_MOST = 256
MICRO = 4
PACKED = 4
MB_TOKENS = 2048


def draw_cross_proj(key, part):
    key = jax.random.fold_in(key, 7)
    noise_draw = jnp.clip(jax.random.normal(key, (2, D, 2 * D), jnp.float32), -6.0, 6.0)
    column = jnp.arange(2 * D)[None, None, :]
    slot_index = jnp.arange(2)[:, None, None]
    is_output = (column // HD % 2 == 1) & (slot_index == 1)
    scaled = noise_draw * jnp.where(is_output, (D // 16) ** (-0.5), D ** (-0.5))
    return scaled.astype(jnp.bfloat16)


def level_of(key, shape, pieces, smallest, top_value):
    gain = 1.0
    for dim, blocks in pieces:
        draws = jax.random.uniform(jax.random.fold_in(jax.random.fold_in(key, 6), dim), (blocks,), jnp.float32, smallest / len(pieces), top_value / len(pieces))
        gain = gain * jnp.repeat(jnp.exp(draws), shape[dim] // blocks).reshape((-1,) + (1,) * (len(shape) - 1 - dim))
    return gain


def profile(amount, total, bound, skew):
    portions = [(1 << 20) // math.isqrt(grade ** skew) + 1 for grade in range(2, amount + 1)]
    spare, holding = total - bound - (amount - 1), [1] * (amount - 1)
    while spare > 0:
        free = [i for i in range(amount - 1) if holding[i] < bound]
        mass, remaining = sum([portions[i] for i in free]), spare
        for i in free:
            addition = min(bound - holding[i], max(1, remaining * portions[i] // mass), spare)
            holding[i] = holding[i] + addition
            spare = spare - addition
    return np.array([bound] + holding)


def ragged_sizes(own_key, count, total, limit, lean):
    if count == 2:
        one = jax.random.randint(own_key, (), max(1, total - limit), min(limit, total - 1) + 1)
        return jnp.stack([one, total - one])
    lengths = jnp.asarray(profile(count, total, limit, lean), jnp.int32)
    twos = (count - 1) // 2
    source_of, taker = lengths[1:1 + 2 * twos:2], lengths[2:2 + 2 * twos:2]
    room = jnp.minimum(source_of - 1, limit - taker)
    passed = jax.random.randint(jax.random.fold_in(own_key, 1), (twos,), 0, 1 << 20) % (room + 1)
    lengths = lengths.at[1:1 + 2 * twos:2].set(source_of - passed).at[2:2 + 2 * twos:2].set(taker + passed)
    return lengths[jax.random.permutation(jax.random.fold_in(own_key, 2), count)]


def centred(key, dims, deviation, reach, pieces=(), held_as=jnp.bfloat16):
    factor_of = level_of(key, dims, pieces, -0.22, 0.18) if pieces else 1.0
    drawn = jax.random.normal(key, dims, jnp.float32) * deviation * factor_of
    return jnp.minimum(jnp.maximum(drawn, -reach), reach).astype(held_as)


def setup_inputs(seed: int = 0) -> dict:
    streams_of = jax.random.split(jax.random.key(seed), 11)
    return {
        "layer_in": centred(streams_of[0], (2, MICRO, MB_TOKENS, D), 1.0, 6.0, ((0, 2), (2, 16))),
        "segments": jax.vmap(lambda own: jnp.searchsorted(jnp.cumsum(ragged_sizes(own, SEGS, LEN, SEG_MOST, 0)), jnp.arange(LEN), side="right"))(jax.random.split(streams_of[1], 2 * MICRO * PACKED)).reshape((2, MICRO, PACKED, LEN)).astype(jnp.int32),
        "cotangent": centred(streams_of[2], (MICRO, MB_TOKENS, D), 1.0, 6.0, ((1, 16),)),
        "self_qkv": centred(streams_of[3], (2, D, 3 * D), D ** -0.5, 0.1875, ((0, 2), (2, 4))),
        "self_out": centred(streams_of[4], (2, D, D), (D // 16) ** -0.5, 0.75, ((0, 2), (1, 4))),
        "cross_proj": draw_cross_proj(jax.random.fold_in(streams_of[10], 71), 0),
        "ffn_up": centred(streams_of[6], (2, D, FF), D ** -0.5, 0.1875, ((0, 2), (2, 4))),
        "ffn_down": centred(streams_of[7], (2, FF, D), FF ** -0.5, 0.09375, ((0, 2), (1, 4))),
        "norm_gain": jnp.clip(1.0 + 0.18 * jax.random.normal(streams_of[8], (2, 3, D), jnp.float32), 0.1, 1.9),
        "norm_bias": centred(streams_of[9], (2, 3, D), 0.3, 1.8, ((0, 2),), jnp.float32),
    }


@jax.custom_vjp
def low(v):
    return lax.optimization_barrier(v.astype(jnp.bfloat16)).astype(jnp.float32)

@jax.custom_vjp
def low_back(v):
    return v

def low_keep(v):
    return (low(v), None)

def low_pass(kept, grad):
    return (grad,)

def back_keep(v):
    return (v, None)

def back_low(kept, grad):
    return (low(grad),)
low.defvjp(low_keep, low_pass)
low_back.defvjp(back_keep, back_low)
eps_norm = 1e-05
masked_score = -1e+30
top_precision = lax.Precision.HIGHEST

def normalize(values, gain_row, bias_row):
    centre = values - lax.optimization_barrier(jnp.mean(values, axis=-1, keepdims=True))
    inv_scale = lax.rsqrt(lax.optimization_barrier(jnp.mean(centre * centre, axis=-1, keepdims=True)) + eps_norm)
    return centre * inv_scale * gain_row + bias_row

def attend_rows(queries, keys_in, values, seg_query, seg_key, causal):

    def one_row(operands):
        query_row, key_row, value_row, seg_qrow, seg_krow = operands
        scores = jnp.einsum('ihe,jhe->hij', query_row, key_row, precision=top_precision) * HD ** (-0.5)
        scores = low_back(scores)
        allowed = seg_qrow[:, None] == seg_krow[None, :]
        if causal:
            positions = jnp.arange(LEN)
            allowed = allowed & (positions[None, :] <= positions[:, None])
        probs_full = jax.nn.softmax(jnp.where(allowed[None], scores, masked_score), axis=-1)
        return jnp.einsum('hij,jhe->ihe', low(probs_full), value_row, precision=top_precision)
    return lax.map(jax.checkpoint(one_row), (queries, keys_in, values, seg_query, seg_key))

def self_block(rows_in, weight_qkv, weight_out, seg_rows, causal):
    row_count = rows_in.shape[0]
    mixed = low_back(low(jnp.dot(low(rows_in), weight_qkv, precision=top_precision)))
    mixed = mixed.reshape(row_count // LEN, LEN, HEADS, 3, HD)
    heads_out = attend_rows(mixed[:, :, :, 0], mixed[:, :, :, 1], mixed[:, :, :, 2], seg_rows, seg_rows, causal)
    heads_out = low_back(low(heads_out.reshape(row_count, D)))
    return low_back(jnp.dot(heads_out, weight_out, precision=top_precision))

def feed_forward(rows_in, weight_up, weight_down):
    hidden_pre = low_back(jnp.dot(low(rows_in), weight_up, precision=top_precision))
    hidden = low(jax.nn.gelu(hidden_pre, approximate=False))
    return low_back(jnp.dot(hidden, weight_down, precision=top_precision))

def forward_micro(weights, enc_rows, dec_rows, seg_pair):
    weight_qkv, weight_out, weight_cross, weight_up, weight_down, gains, biases = weights
    enc_segs = seg_pair[0]
    dec_segs = seg_pair[1]
    row_count = enc_rows.shape[0]
    start = normalize(enc_rows, gains[0, 1], biases[0, 1])
    after_self = normalize(start + self_block(start, weight_qkv[0], weight_out[0], enc_segs, False), gains[0, 0], biases[0, 0])
    memory = normalize(after_self + feed_forward(after_self, weight_up[0], weight_down[0]), gains[0, 2], biases[0, 2])
    cross_enc = weight_cross[0].reshape(D, HEADS, 2, HD)
    cross_dec = weight_cross[1].reshape(D, HEADS, 2, HD)
    key_value = low_back(low(jnp.einsum('nd,dhje->nhje', low(memory), cross_enc, precision=top_precision)))
    key_value = key_value.reshape(row_count // LEN, LEN, HEADS, 2, HD)
    dec_self = normalize(dec_rows + self_block(dec_rows, weight_qkv[1], weight_out[1], dec_segs, True), gains[1, 0], biases[1, 0])
    queries = low_back(low(jnp.einsum('nd,dhe->nhe', low(dec_self), cross_dec[:, :, 0], precision=top_precision)))
    queries = queries.reshape(row_count // LEN, LEN, HEADS, HD)
    cross_out = attend_rows(queries, key_value[:, :, :, 0], key_value[:, :, :, 1], dec_segs, enc_segs, False)
    cross_out = low_back(low(cross_out.reshape(row_count, HEADS, HD)))
    cross_mix = low_back(jnp.einsum('nhe,dhe->nd', cross_out, cross_dec[:, :, 1], precision=top_precision))
    after_cross = normalize(dec_self + cross_mix, gains[1, 1], biases[1, 1])
    decoded = normalize(after_cross + feed_forward(after_cross, weight_up[1], weight_down[1]), gains[1, 2], biases[1, 2])
    return (memory, decoded)

def reference(layer_in, segments, cotangent, self_qkv, self_out, cross_proj, ffn_up, ffn_down, norm_gain, norm_bias):
    weights = (self_qkv.astype(jnp.float32), self_out.astype(jnp.float32), cross_proj.astype(jnp.float32), ffn_up.astype(jnp.float32), ffn_down.astype(jnp.float32), norm_gain.astype(jnp.float32), norm_bias.astype(jnp.float32))
    inputs = layer_in.astype(jnp.float32)
    cot_all = cotangent.astype(jnp.float32)
    seg_micro = jnp.moveaxis(segments, 1, 0)

    def one_micro(totals, operands):
        enc_rows, dec_rows, seg_pair, cot_rows = operands
        outs_pair, pull_back = jax.vjp(partial(forward_micro, seg_pair=seg_pair), weights, enc_rows, dec_rows)
        memory, decoded = outs_pair
        grad_weights, grad_enc, grad_dec = pull_back((jnp.zeros_like(memory), cot_rows))
        totals = jax.tree.map(jnp.add, totals, grad_weights)
        return (totals, (memory.astype(jnp.bfloat16), decoded.astype(jnp.bfloat16), grad_enc.astype(jnp.bfloat16), grad_dec.astype(jnp.bfloat16)))
    zero_totals = jax.tree.map(jnp.zeros_like, weights)
    totals, stacked = lax.scan(one_micro, zero_totals, (inputs[0], inputs[1], seg_micro, cot_all))
    memories, decodeds, grad_encs, grad_decs = stacked
    layer_out = jnp.stack([memories, decodeds])
    input_grad = jnp.stack([grad_encs, grad_decs])
    return (layer_out, input_grad, totals[0], totals[1], totals[2], totals[3], totals[4], totals[5], totals[6])
```

```python
import math

import jax
import jax.numpy as jnp
from jax import lax
from jax.experimental import pallas as pl
from jax.experimental.pallas import tpu as pltpu
from jax.sharding import PartitionSpec as P

HD = 64
EPS = 1e-05
MASKED = -1e30
BF = jnp.bfloat16
F32 = jnp.float32
VMEM_SPARE = 6 * 1024 * 1024
GELU_C = 0.7071067811865476
PHI_C = 0.3989422804014327


LIGHT = pl.CostEstimate(flops=1024, bytes_accessed=1024, transcendentals=0)


def mm(a, b):
    return jnp.dot(a, b, preferred_element_type=F32)


def mm_bt(a, b):
    return lax.dot_general(a, b, (((1,), (1,)), ((), ())), preferred_element_type=F32)


def mm_at(a, b):
    return lax.dot_general(a, b, (((0,), (0,)), ((), ())), preferred_element_type=F32)


def spec(shape, dtype=BF):
    return jax.ShapeDtypeStruct(shape, dtype)


class Saved:
    def __init__(self, shape, dtype=BF):
        self.shape, self.dtype, self.size = shape, jnp.dtype(dtype), math.prod(shape)


def in_hbm(array):
    return pltpu.with_memory_space_constraint(array, pltpu.HBM)


class Near:
    def __init__(self, shape, p, q=None, at=0):
        self.shape, self.p, self.q, self.at = shape, p, q, at
        self.dtype, self.size = p.dtype, shape[0] * shape[1]


STRICT = [True]
ORDER = []


def in_order(deps):
    return (*deps, *ORDER[-1:]) if STRICT[-1] else tuple(deps)


def note(results):
    ORDER.append(results[0] if isinstance(results, (tuple, list)) else results)
    return results


def sectioned(
    body, core, flags, small, big, outs, scratch, flops, trans=0, deps=(), owners=None, sums=()
):
    deps = in_order(deps)
    terms = [array for chain in sums for array in (chain.value, chain.got)]
    n_terms = len(terms)
    sources, places = [], []
    for i, array in enumerate(big):
        if isinstance(array, Near) and array.q is None:
            places.append((i, array.shape[0], array.at, None))
            sources.append(array.p)
        elif isinstance(array, Near):
            half = array.shape[0] // 2
            for turn, part in enumerate((array.p, array.q)):
                places.append((i, half, array.at, turn))
                sources.append(part)
        else:
            places.append((i, None, None, None))
            sources.append(array)
    n_small, n_big, n_deps, n_out = len(small), len(big), len(deps), len(outs)
    n_src = len(sources)

    def kernel(flags_ref, *refs):
        small_refs = refs[:n_small]
        big_hbm = refs[n_small : n_small + n_src]
        at = n_small + n_src
        term_hbm = refs[at : at + n_terms]
        at += n_terms + n_deps
        out_hbm = refs[at : at + n_out]
        at += n_out
        sum_hbm = refs[at : at + len(sums)]
        at += len(sums)
        big_refs = refs[at : at + n_big]
        at += n_big
        out_refs = refs[at : at + n_out]
        at += n_out
        term_refs = refs[at : at + n_terms]
        at += n_terms
        extra = refs[at:-4]
        in_sem, out_sem, term_sem, sum_sem = refs[-4:]

        def start_sums():
            loads = [
                pltpu.make_async_copy(term_hbm[i], term_refs[i], term_sem.at[i])
                for i in range(n_terms)
            ]
            for load in loads:
                load.start()
            return loads

        def end_sums(loads):
            stores = []
            for i in range(len(sums)):
                loads[2 * i].wait()
                loads[2 * i + 1].wait()
                a_ref, b_ref = term_refs[2 * i], term_refs[2 * i + 1]
                chunk = 64 if a_ref.shape[0] % 64 == 0 else a_ref.shape[0]

                @pl.loop(0, a_ref.shape[0] // chunk)
                def _(r):
                    at = pl.ds(pl.multiple_of(r * chunk, chunk), chunk)
                    a_ref[at, :] = (a_ref[at, :].astype(F32) + b_ref[at, :].astype(F32)).astype(BF)

                stores.append(pltpu.make_async_copy(a_ref, sum_hbm[i], sum_sem.at[i]))
                stores[-1].start()
            return stores

        def run():
            copies = [[] for _ in range(n_big)]
            for s, (i, half, first, turn) in enumerate(places):
                if half is None:
                    copy = pltpu.make_async_copy(big_hbm[s], big_refs[i], in_sem.at[s])
                elif turn is None:
                    copy = pltpu.make_async_copy(
                        big_hbm[s].at[pl.ds(first, half), :], big_refs[i], in_sem.at[s]
                    )
                else:
                    odd = flags_ref[1] if turn == 0 else 1 - flags_ref[1]
                    copy = pltpu.make_async_copy(
                        big_hbm[s].at[pl.ds(first, half), :],
                        big_refs[i].at[pl.ds(pl.multiple_of(odd * half, half), half), :],
                        in_sem.at[s],
                    )
                if owners is None:
                    copy.start()
                else:
                    pl.when(flags_ref[0] == owners[i])(copy.start)
                copies[i].append(copy)
            done = [
                pltpu.make_async_copy(out_refs[i], out_hbm[i], out_sem.at[i]) for i in range(n_out)
            ]
            loads = start_sums() if sums and core is not None else None
            body(
                flags_ref, small_refs, big_refs, out_refs, extra,
                lambda *which: [copy.wait() for i in which for copy in copies[i]],
                lambda *which: [done[i].start() for i in which],
            )
            if loads:
                done.extend(end_sums(loads))
            for copy in done:
                copy.wait()

        if core is None:
            run()
        else:
            pl.when(flags_ref[0] == core)(run)
        if sums and core is None:

            @pl.when(flags_ref[0] == sums[0].core)
            def _():
                for copy in end_sums(start_sums()):
                    copy.wait()

    nbytes = sum(a.size * a.dtype.itemsize for a in (*big, *outs))
    nbytes += sum(a.size * 2 for a in terms)
    held = nbytes + sum(math.prod(a.shape) * jnp.dtype(a.dtype).itemsize for a in scratch)
    results = note(pl.pallas_call(
        kernel,
        out_shape=tuple(pltpu.HBM(a.shape, a.dtype) if isinstance(a, Saved) else a for a in outs)
        + tuple(spec(chain.value.shape) for chain in sums),
        in_specs=[pl.BlockSpec(memory_space=pltpu.SMEM)]
        + [pl.BlockSpec(memory_space=pltpu.VMEM)] * n_small
        + [pl.BlockSpec(memory_space=pl.ANY)] * (n_src + n_terms + n_deps),
        out_specs=tuple(
            pl.BlockSpec(memory_space=pltpu.HBM if isinstance(a, Saved) else pl.ANY) for a in outs
        )
        + tuple([pl.BlockSpec(memory_space=pl.ANY)] * len(sums)),
        scratch_shapes=[pltpu.VMEM(a.shape, a.dtype) for a in (*big, *outs)]
        + [pltpu.VMEM(a.shape, BF) for a in terms]
        + list(scratch)
        + [
            pltpu.SemaphoreType.DMA((max(1, n_src),)), pltpu.SemaphoreType.DMA((n_out,)),
            pltpu.SemaphoreType.DMA((max(1, n_terms),)),
            pltpu.SemaphoreType.DMA((max(1, len(sums)),)),
        ],
        compiler_params=pltpu.CompilerParams(vmem_limit_bytes=int(held) + VMEM_SPARE),
        cost_estimate=LIGHT,
    )(flags, *small, *sources, *terms, *deps))
    for chain, value in zip(sums, results[n_out:]):
        chain.forward(value)
    return results[:n_out]


def norm_rows(terms, gain, bias, x_ref, hat_ref, inv_ref, chunk=32):
    rows, width = x_ref.shape

    @pl.loop(0, rows // chunk, unroll=4)
    def _(i):
        at = pl.ds(pl.multiple_of(i * chunk, chunk), chunk)
        v = sum(term[at, :].astype(F32) for term in terms)
        centre = v - jnp.mean(v, axis=-1, keepdims=True)
        inv = lax.rsqrt(jnp.mean(centre * centre, axis=-1, keepdims=True) + EPS)
        hat = centre * inv
        x_ref[at, :] = (hat * gain[...] + bias[...]).astype(BF)
        if hat_ref is not None:
            hat_ref[at, :] = hat.astype(BF)
            inv_ref[at, :] = jnp.broadcast_to(inv, (chunk, 128))


def norm_back_rows(terms, hat_ref, inv_ref, gain, dv_ref, n_ref, chunk=32):
    rows, width = dv_ref.shape

    def step(i, sums):
        at = pl.ds(pl.multiple_of(i * chunk, chunk), chunk)
        dy = sum(term[at, :].astype(F32) for term in terms)
        hat = hat_ref[at, :].astype(F32)
        t = dy * gain[...]
        dv = (
            t
            - jnp.mean(t, axis=-1, keepdims=True)
            - hat * jnp.mean(t * hat, axis=-1, keepdims=True)
        ) * inv_ref[at, :1]
        dv_ref[at, :] = dv.astype(BF)
        return (
            sums[0] + (dy * hat).reshape(chunk // 8, 8, width).sum(0),
            sums[1] + dy.reshape(chunk // 8, 8, width).sum(0),
        )

    zero = jnp.zeros((8, width), F32)
    n_ref[0], n_ref[1] = lax.fori_loop(0, rows // chunk, step, (zero, zero), unroll=4)


def matmul_into(x_ref, w_ref, out_ref, at=0, tile=256):
    columns = w_ref.shape[1]
    tile = min(tile, columns)
    for c in range(0, columns, tile):
        out_ref[:, at + c : at + c + tile] = mm(x_ref[...], w_ref[:, c : c + tile]).astype(BF)


def matmul_bt_into(x_ref, w_ref, out_ref, at=0, tile=256):
    rows = w_ref.shape[0]
    tile = min(tile, rows)
    for c in range(0, rows, tile):
        out_ref[:, at + c : at + c + tile] = mm_bt(x_ref[...], w_ref[c : c + tile, :]).astype(BF)


def attend(heads, length, step, offsets, o_step, causal, q_ref, kv_ref, segq, segk, o_ref, lse_ref, bias_ref):
    q_off, k_off, v_off, o_off = offsets
    tile = min(256, length)
    if o_step != HD:
        o_ref[...] = jnp.zeros_like(o_ref)
    lse_ref[...] = jnp.zeros_like(lse_ref)
    for p in range(q_ref.shape[0] // length):
        base = p * length
        all_rows = slice(base, base + length)
        same = segq[all_rows, :] == segk[p : p + 1, :]
        if causal is not None:
            rows = lax.broadcasted_iota(jnp.int32, (length, length), 0)
            cols = lax.broadcasted_iota(jnp.int32, (length, length), 1)
            same = same & (cols * causal <= rows)
        bias_ref[...] = jnp.where(same, 0.0, MASKED)
        for h in range(heads):
            k = kv_ref[all_rows, h * step + k_off : h * step + k_off + HD]
            v = kv_ref[all_rows, h * step + v_off : h * step + v_off + HD]
            for r in range(0, length, tile):
                at = slice(base + r, base + r + tile)
                q = q_ref[at, h * step + q_off : h * step + q_off + HD] * jnp.asarray(HD**-0.5, BF)
                s = mm_bt(q, k) + bias_ref[r : r + tile, :]
                top = jnp.max(s, axis=-1, keepdims=True)
                e = jnp.exp(s - top)
                total = jnp.sum(e, axis=-1, keepdims=True)
                prob = (e * (1.0 / total)).astype(BF)
                o_ref[at, h * o_step + o_off : h * o_step + o_off + HD] = mm(prob, v).astype(BF)
                lse_ref[at, h : h + 1] = top + jnp.log(total)


def attend_back(
    heads, length, step, offsets, o_step, causal, q_ref, kv_ref, segq, segk, o_ref, lse_ref, do_ref,
    dq_ref, dkv_ref, bias_ref, inner_ref,
):
    q_off, k_off, v_off, o_off = offsets
    tile = min(256, length)
    if dq_ref is not dkv_ref:
        dq_ref[...] = jnp.zeros_like(dq_ref)
    for p in range(q_ref.shape[0] // length):
        base = p * length
        all_rows = slice(base, base + length)
        same = segk[all_rows, :] == segq[p : p + 1, :]
        if causal is not None:
            keys = lax.broadcasted_iota(jnp.int32, (length, length), 0)
            queries = lax.broadcasted_iota(jnp.int32, (length, length), 1)
            same = same & (keys * causal <= queries)
        bias_ref[...] = jnp.where(same, 0.0, MASKED)
        inner_ref[...] = jnp.zeros_like(inner_ref)
        for h in range(heads):
            cols = slice(h * o_step + o_off, h * o_step + o_off + HD)
            prod = do_ref[all_rows, cols].astype(F32) * o_ref[all_rows, cols].astype(F32)
            inner_ref[:, h : h + 1] = jnp.sum(prod, axis=-1, keepdims=True)
        inner_t = jnp.transpose(inner_ref[...])
        lse_t = jnp.transpose(lse_ref[all_rows, :])
        for h in range(heads):
            q_cols = slice(h * step + q_off, h * step + q_off + HD)
            k_cols = slice(h * step + k_off, h * step + k_off + HD)
            v_cols = slice(h * step + v_off, h * step + v_off + HD)
            q = q_ref[all_rows, q_cols] * jnp.asarray(HD**-0.5, BF)
            do = do_ref[all_rows, h * o_step + o_off : h * o_step + o_off + HD]
            dq = jnp.zeros((length, HD), F32)
            for r in range(0, length, tile):
                rows = slice(base + r, base + r + tile)
                k = kv_ref[rows, k_cols]
                v = kv_ref[rows, v_cols]
                s = mm_bt(k, q) + bias_ref[r : r + tile, :]
                prob = jnp.exp(s - lse_t[h : h + 1, :])
                dkv_ref[rows, v_cols] = mm(prob.astype(BF), do).astype(BF)
                ds = (prob * (mm_bt(v, do) - inner_t[h : h + 1, :])).astype(BF)
                dkv_ref[rows, k_cols] = mm(ds, q).astype(BF)
                dq = dq + mm_at(ds, k)
            dq_ref[all_rows, q_cols] = (dq * HD**-0.5).astype(BF)


SELF_AT = (0, HD, 2 * HD, 0)
CROSS_AT = (0, 0, HD, HD)


def self_forward(flags, src, seg, gain, bias, w_qkv, w_out, deps=()):
    packed, length = seg.shape
    rows, width = src.shape
    heads = 2 * w_out[0].shape[0] // HD
    part = w_qkv[0].shape[1]

    def body(flags, small, big, outs, extra, wait, flush):
        segq, segk, gain, bias = small
        src, qkv_a, qkv_b, out_a, out_b = big
        x, hat, inv, qkv, o, lse, partial = outs
        (mask,) = extra
        wait(0)

        @pl.when(flags[0] == 0)
        def _():
            norm_rows([src], gain, bias, x, hat, inv)

        @pl.when(flags[0] != 0)
        def _():
            x[...] = src[...]

        flush(0, 1, 2)
        wait(1)
        matmul_into(x, qkv_a, qkv)
        wait(2)
        matmul_into(x, qkv_b, qkv, part)
        flush(3)
        attend(heads, length, 3 * HD, SELF_AT, HD, flags[0], qkv, qkv, segq, segk, o, lse, mask)
        flush(4, 5)
        wait(3, 4)
        half = heads // 2 * HD
        for c in range(0, width, 256):
            partial[:, c : c + 256] = (
                mm(o[:, :half], out_a[:, c : c + 256]) + mm(o[:, half:], out_b[:, c : c + 256])
            ).astype(BF)
        flush(6)

    return sectioned(
        body, None, flags,
        (seg.reshape(rows, 1), seg, gain, bias),
        (src, *w_qkv, *w_out),
        (
            spec((rows, width)), Saved((rows, width)), Saved((rows, 128), F32),
            Saved((rows, 2 * part)), Saved((rows, heads * HD)), Saved((rows, 128), F32),
            spec((rows, width)),
        ),
        [pltpu.VMEM((length, length), F32)],
        2 * rows * width * heads * HD * 4 + 16 * heads * rows * length * HD,
        heads * rows * length, deps,
    )


def ffn_forward(core, flags, res, pair, gain, bias, w_up, w_down, deps=()):
    rows, width = res.shape
    part = w_up[0].shape[1]
    tile = min(512, part)

    def body(flags, small, big, outs, extra, wait, flush):
        gain, bias = small
        res, own, got, up_a, up_b, down_a, down_b = big
        x, hat, inv, hidden, slope, partial = outs
        (total,) = extra
        wait(0, 1, 2)
        norm_rows([res, own, got], gain, bias, x, hat, inv)
        flush(0, 1, 2)
        for i, (up, down) in enumerate(((up_a, down_a), (up_b, down_b))):
            wait(3 + i, 5 + i)
            for c in range(0, part, tile):
                at = slice(i * part + c, i * part + c + tile)
                u = mm(x[...], up[:, c : c + tile])
                phi = 0.5 * (1.0 + lax.erf(u * GELU_C))
                slope[:, at] = (phi + u * (PHI_C * jnp.exp(-0.5 * u * u))).astype(BF)
                hidden[:, at] = (u * phi).astype(BF)
                term = mm(hidden[:, at], down[c : c + tile, :])
                if i == 0 and c == 0:
                    total[...] = term
                else:
                    total[...] += term
        partial[...] = total[...].astype(BF)
        flush(3, 4, 5)

    return sectioned(
        body, core, flags, (gain, bias), (res, *pair, *w_up, *w_down),
        (
            spec((rows, width)), Saved((rows, width)), Saved((rows, 128), F32),
            Saved((rows, 2 * part)), Saved((rows, 2 * part)), spec((rows, width)),
        ),
        [pltpu.VMEM((rows, width), F32)],
        8 * rows * width * part, rows * part * 4, deps,
    )


def norm_project(core, flags, res, pair, gain, bias, w, deps=()):
    rows, width = res.shape
    part = w[0].shape[1]

    def body(flags, small, big, outs, extra, wait, flush):
        gain, bias = small
        res, own, got, w_a, w_b = big
        x, hat, inv, proj = outs
        wait(0, 1, 2)
        norm_rows([res, own, got], gain, bias, x, hat, inv)
        flush(0, 1, 2)
        wait(3)
        matmul_into(x, w_a, proj)
        wait(4)
        matmul_into(x, w_b, proj, part)
        flush(3)

    return sectioned(
        body, core, flags, (gain, bias), (res, *pair, *w),
        (spec((rows, width)), Saved((rows, width)), Saved((rows, 128), F32), spec((rows, 2 * part))),
        [], 4 * rows * width * part, 0, deps,
    )


def cross_forward(core, flags, q, kv, segq, segk, w, deps=()):
    packed, length = segq.shape
    rows = q.shape[0]
    width, part = w[0].shape
    heads = 2 * part // (2 * HD)

    def body(flags, small, big, outs, extra, wait, flush):
        segq, segk = small
        q, kv, w_a, w_b = big
        c, lse, partial = outs
        (mask,) = extra
        wait(0, 1)
        attend(heads, length, 2 * HD, CROSS_AT, 2 * HD, None, q, kv, segq, segk, c, lse, mask)
        flush(0, 1)
        wait(2, 3)
        for r in range(0, width, 256):
            partial[:, r : r + 256] = (
                mm_bt(c[:, :part], w_a[r : r + 256, :]) + mm_bt(c[:, part:], w_b[r : r + 256, :])
            ).astype(BF)
        flush(2)

    return sectioned(
        body, core, flags, (segq.reshape(rows, 1), segk), (q, kv, *w),
        (Saved((rows, 2 * part)), Saved((rows, 128), F32), spec((rows, width))),
        [pltpu.VMEM((length, length), F32)],
        4 * rows * width * part + 16 * heads * rows * length * HD, heads * rows * length, deps,
    )


def ffn_back_loop(df, slope, up, down, du, total, partial, wait, first):
    part = up[0].shape[1]
    tile = min(512, part)
    for i in range(2):
        wait(first + i, first + 2 + i)
        for c in range(0, part, tile):
            at = slice(i * part + c, i * part + c + tile)
            dh = mm_bt(df[...], down[i][c : c + tile, :])
            du[:, at] = (dh * slope[:, at].astype(F32)).astype(BF)
            term = mm_bt(du[:, at], up[i][:, c : c + tile])
            if i == 0 and c == 0:
                total[...] = term
            else:
                total[...] += term
    partial[...] = total[...].astype(BF)


def top_backward(core, flags, res, pair, cot, gain, bias, slope, w_up, w_down, deps=()):
    rows, width = res.shape
    part = w_up[0].shape[1]

    def body(flags, small, big, outs, extra, wait, flush):
        gain, bias = small
        res, own, got, cot, slope, up_a, up_b, down_a, down_b = big
        y, df, n, du, partial = outs
        total, hat, inv = extra
        wait(0, 1, 2)
        norm_rows([res, own, got], gain, bias, y, hat, inv)
        flush(0)
        wait(3)
        norm_back_rows([cot], hat, inv, gain, df, n)
        flush(1, 2)
        wait(4)
        ffn_back_loop(df, slope, (up_a, up_b), (down_a, down_b), du, total, partial, wait, 5)
        flush(3, 4)

    return sectioned(
        body, core, flags, (gain, bias), (res, *pair, in_hbm(cot), in_hbm(slope), *w_up, *w_down),
        (
            Saved((rows, width)), spec((rows, width)), Saved((2, 8, width), F32),
            Saved((rows, 2 * part)), spec((rows, width)),
        ),
        [pltpu.VMEM((rows, width), F32), pltpu.VMEM((rows, width), BF), pltpu.VMEM((rows, 128), F32)],
        8 * rows * width * part, 0, deps,
    )


def ffn_backward(core, flags, terms, kept, gain, slope, w_up, w_down, deps=()):
    rows, width = terms[0].shape
    part = w_up[0].shape[1]
    k = len(terms)

    def body(flags, small, big, outs, extra, wait, flush):
        (gain,) = small
        terms = big[:k]
        hat, inv, slope, up_a, up_b, down_a, down_b = big[k:]
        df, n, du, partial = outs
        (total,) = extra
        wait(*range(k + 2))
        norm_back_rows(terms, hat, inv, gain, df, n)
        flush(0, 1)
        wait(k + 2)
        ffn_back_loop(df, slope, (up_a, up_b), (down_a, down_b), du, total, partial, wait, k + 3)
        flush(2, 3)

    return sectioned(
        body, core, flags, (gain,), (*terms, *map(in_hbm, kept), in_hbm(slope), *w_up, *w_down),
        (
            spec((rows, width)), Saved((2, 8, width), F32), Saved((rows, 2 * part)),
            spec((rows, width)),
        ),
        [pltpu.VMEM((rows, width), F32)],
        8 * rows * width * part, 0, deps,
    )


def cross_backward(core, flags, terms, kept, gain, q, kv, segq, segk, c, lse, w, deps=()):
    packed, length = segq.shape
    rows, width = terms[0].shape
    part = w[0].shape[1]
    heads = 2 * part // (2 * HD)
    k = len(terms)

    def body(flags, small, big, outs, extra, wait, flush):
        segq, segk, gain = small
        terms = big[:k]
        hat, inv, w_a, w_b, q, kv, c, lse = big[k:]
        dca, n, dq, dkv, partial = outs
        dc, mask, inner = extra
        wait(*range(k + 2))
        norm_back_rows(terms, hat, inv, gain, dca, n)
        flush(0, 1)
        wait(k + 2, k + 3)
        matmul_into(dca, w_a, dc)
        matmul_into(dca, w_b, dc, part)
        wait(*range(k + 4, k + 8))
        attend_back(
            heads, length, 2 * HD, CROSS_AT, 2 * HD, None, q, kv, segq, segk, c, lse, dc, dq, dkv,
            mask, inner,
        )
        flush(2, 3)
        for r in range(0, width, 256):
            partial[:, r : r + 256] = (
                mm_bt(dq[:, :part], w_a[r : r + 256, :]) + mm_bt(dq[:, part:], w_b[r : r + 256, :])
            ).astype(BF)
        flush(4)

    return sectioned(
        body, core, flags, (segq, segk.reshape(rows, 1), gain),
        (*terms, *map(in_hbm, kept), *w, *map(in_hbm, (q, kv, c, lse))),
        (
            spec((rows, width)), Saved((2, 8, width), F32), Saved((rows, 2 * part)),
            spec((rows, 2 * part)), spec((rows, width)),
        ),
        [
            pltpu.VMEM((rows, 2 * part), BF), pltpu.VMEM((length, length), F32),
            pltpu.VMEM((length, 128), F32),
        ],
        8 * rows * width * part + 40 * heads * rows * length * HD, heads * rows * length, deps,
    )


def memory_backward(core, flags, dkv, w, deps=()):
    rows = dkv.shape[0]
    width, part = w[0].shape

    def body(flags, small, big, outs, extra, wait, flush):
        dkv, w_a, w_b = big
        (partial,) = outs
        wait(0, 1, 2)
        for r in range(0, width, 256):
            partial[:, r : r + 256] = (
                mm_bt(dkv[:, :part], w_a[r : r + 256, :]) + mm_bt(dkv[:, part:], w_b[r : r + 256, :])
            ).astype(BF)
        flush(0)

    return sectioned(
        body, core, flags, (), (dkv, *w), (spec((rows, width)),), [], 4 * rows * width * part, 0, deps
    )[0]


def self_backward(
    core, flags, terms, kept, gain, qkv, o, lse, seg, w_qkv, w_out, deps=(), sums=()
):
    packed, length = seg.shape
    rows, width = terms[0].shape
    heads = 2 * w_out[0].shape[0] // HD
    part = w_qkv[0].shape[1]
    k = len(terms)

    def body(flags, small, big, outs, extra, wait, flush):
        segq, segk, gain = small
        terms = big[:k]
        hat, inv, out_a, out_b, qkv, o, lse, qkv_a, qkv_b = big[k:]
        ds, n, dqkv, partial = outs
        do, mask, inner = extra
        wait(*range(k + 2))
        norm_back_rows(terms, hat, inv, gain, ds, n)
        flush(0, 1)
        wait(k + 2, k + 3)
        half = heads // 2 * HD
        matmul_bt_into(ds, out_a, do)
        matmul_bt_into(ds, out_b, do, half)
        wait(*range(k + 4, k + 7))
        attend_back(
            heads, length, 3 * HD, SELF_AT, HD, flags[0], qkv, qkv, segq, segk, o, lse, do, dqkv,
            dqkv, mask, inner,
        )
        flush(2)
        wait(k + 7, k + 8)
        for r in range(0, width, 256):
            partial[:, r : r + 256] = (
                mm_bt(dqkv[:, :part], qkv_a[r : r + 256, :])
                + mm_bt(dqkv[:, part:], qkv_b[r : r + 256, :])
            ).astype(BF)
        flush(3)

    return sectioned(
        body, core, flags, (seg, seg.reshape(rows, 1), gain),
        (*terms, *map(in_hbm, kept), *w_out, *map(in_hbm, (qkv, o, lse)), *w_qkv),
        (
            spec((rows, width)), Saved((2, 8, width), F32), Saved((rows, 2 * part)),
            spec((rows, width)),
        ),
        [
            pltpu.VMEM((rows, heads * HD), BF), pltpu.VMEM((length, length), F32),
            pltpu.VMEM((length, 128), F32),
        ],
        2 * rows * width * heads * HD * 4 + 40 * heads * rows * length * HD,
        heads * rows * length, deps, sums=sums,
    )


def weight_grads(flags, groups, deps=(), cuts=1, sums=()):
    lists = [
        in_hbm(array) for own in groups for lefts, rights, _ in own for array in (*lefts, *rights)
    ]
    live = [core for core in range(2) if groups[core]]
    some = groups[live[0]]
    height = some[0][0][0].shape[1] // (2 if some[0][2] else 1)
    widths = [
        [rights[0].shape[1] // (1 if split_left else 2) for _, rights, split_left in own]
        for own in groups
    ]
    piece = height // cuts
    counts = [sum(2 * len(lefts) for lefts, _, _ in own) for own in groups]

    def body(flags, small, big, outs, extra, wait, flush):
        def run(core):
            for i in reversed(range(2)):
                first, at = counts[0] * core, 0
                for g, (lefts, rights, split_left) in enumerate(groups[core]):
                    k = len(lefts)
                    if i == 1:
                        wait(*range(first, first + 2 * k))
                    i_m = i * height if split_left else 0
                    n = widths[core][g]
                    i_n = 0 if split_left else i * n
                    tile = min(256, piece)
                    for r in range(0, height, tile):
                        low = r % piece
                        outs[i * cuts + r // piece][low : low + tile, at : at + n] = sum(
                            mm_at(
                                big[first + j][:, i_m + r : i_m + r + tile],
                                big[first + k + j][:, i_n : i_n + n],
                            )
                            for j in range(k)
                        ).astype(BF)
                    first += 2 * k
                    at += n
                flush(*range(i * cuts, (i + 1) * cuts))

        if len(live) == 1:
            run(live[0])
        else:
            for core in live:
                pl.when(flags[0] == core)(lambda core=core: run(core))

    blocks = tuple(spec((piece, sum(widths[live[0]]))) for _ in range(2 * cuts))
    owners = [0] * counts[0] + [1] * counts[1]
    return sectioned(
        body, live[0] if len(live) == 1 else None, flags, (), lists, blocks, [], 0, 0, deps, owners,
        sums,
    )


def after(array, *deps):
    deps = in_order(deps)
    return note(pl.pallas_call(
        lambda *refs: None,
        out_shape=spec(array.shape, array.dtype),
        in_specs=[pl.BlockSpec(memory_space=pl.ANY)] * (1 + len(deps)),
        out_specs=pl.BlockSpec(memory_space=pl.ANY),
        input_output_aliases={0: 0},
        cost_estimate=LIGHT,
    )(array, *deps))


def pack_rows(flags, weights, deps=(), whole=False):
    deps = in_order(deps)
    halves = [w.shape[0] // (1 if whole else 2) for w in weights]
    out = spec((sum(halves), weights[0].shape[1]))

    def kernel(flags_ref, *refs):
        target, sem = refs[-2:]
        copies, at = [], 0
        for i, half in enumerate(halves):
            first = 0 if whole else pl.multiple_of(flags_ref[1] * half, half)
            copies.append(
                pltpu.make_async_copy(
                    refs[i].at[pl.ds(first, half), :], target.at[pl.ds(at, half), :], sem.at[i]
                )
            )
            at += half
        for copy in copies:
            copy.start()
        for copy in copies:
            copy.wait()

    return note(pl.pallas_call(
        kernel,
        out_shape=out,
        in_specs=[pl.BlockSpec(memory_space=pltpu.SMEM)]
        + [pl.BlockSpec(memory_space=pl.ANY)] * (len(weights) + len(deps)),
        out_specs=pl.BlockSpec(memory_space=pltpu.VMEM),
        scratch_shapes=[pltpu.SemaphoreType.DMA((len(weights),))],
        cost_estimate=LIGHT,
    )(flags, *weights, *deps))


def add_pairs(flags, pairs, deps=()):
    deps = in_order(deps)
    k = len(pairs)
    cuts = [4 if a.shape[0] % 64 == 0 else 1 for _, a, _ in pairs]

    def kernel(flags_ref, *refs):
        terms = refs[: 2 * k]
        outs = refs[2 * k + len(deps) : 3 * k + len(deps)]
        held = refs[3 * k + len(deps) : -2]
        in_sem, out_sem = refs[-2:]
        jobs = []
        for p, (core, a, _) in enumerate(pairs):
            live = flags_ref[0] >= 0 if core is None else flags_ref[0] == core
            chunk = a.shape[0] // cuts[p]
            for i in range(cuts[p]):
                at = pl.ds(i * chunk, chunk)
                loads = [
                    pltpu.make_async_copy(
                        terms[2 * p + j].at[at, :], held[2 * p + j].at[at, :], in_sem.at[2 * p + j, i]
                    )
                    for j in range(2)
                ]
                store = pltpu.make_async_copy(held[2 * p].at[at, :], outs[p].at[at, :], out_sem.at[p, i])
                jobs.append((live, at, held[2 * p], held[2 * p + 1], loads, store))
        for live, _, _, _, loads, _ in jobs:

            @pl.when(live)
            def _():
                for load in loads:
                    load.start()

        for live, at, a_ref, b_ref, loads, store in jobs:

            @pl.when(live)
            def _():
                for load in loads:
                    load.wait()
                a_ref[at, :] = (a_ref[at, :].astype(F32) + b_ref[at, :].astype(F32)).astype(BF)
                store.start()

        for live, _, _, _, _, store in jobs:
            pl.when(live)(store.wait)

    arrays = [array for _, a, b in pairs for array in (a, b)]
    return note(pl.pallas_call(
        kernel,
        out_shape=tuple(spec(a.shape) for _, a, _ in pairs),
        in_specs=[pl.BlockSpec(memory_space=pltpu.SMEM)]
        + [pl.BlockSpec(memory_space=pl.ANY)] * (2 * k + len(deps)),
        out_specs=tuple([pl.BlockSpec(memory_space=pl.ANY)] * k),
        scratch_shapes=[pltpu.VMEM(array.shape, BF) for array in arrays]
        + [pltpu.SemaphoreType.DMA((2 * k, 4)), pltpu.SemaphoreType.DMA((k, 4))],
        compiler_params=pltpu.CompilerParams(
            vmem_limit_bytes=sum(2 * array.size for array in arrays) + VMEM_SPARE
        ),
        cost_estimate=LIGHT,
    )(flags, *arrays, *deps))


def finish(flags, kept, got, columns, deps=()):
    deps = in_order(deps)
    sources = [kept[0], kept[1], got[0], got[1]]
    rows = sum(piece.shape[0] for piece in sources[0][0])
    cuts = 4 if rows % 64 == 0 else max(len(pieces) for pieces, _ in sources)
    chunk = rows // cuts
    flat = [piece for pieces, _ in sources for piece in pieces]

    def kernel(flags_ref, *refs):
        out_hbm, low_ref, out_ref, in_sem, out_sem = refs[len(flat) + len(deps) :]
        loads, stores = [], []
        for i in range(cuts):
            at = pl.ds(i * chunk, chunk)
            first_ref = 0
            for c, (pieces, first) in enumerate(sources):
                size = rows // len(pieces)
                load = pltpu.make_async_copy(
                    refs[first_ref + i * chunk // size].at[
                        pl.ds(i * chunk % size, chunk), pl.ds(first, columns)
                    ],
                    low_ref.at[at, :],
                    in_sem.at[i],
                )
                pl.when(flags_ref[0] + 2 * flags_ref[2] == c)(load.start)
                first_ref += len(pieces)
            loads.append(load)
            stores.append(pltpu.make_async_copy(out_ref.at[at, :], out_hbm.at[at, :], out_sem.at[i]))
        for i in range(cuts):
            at = pl.ds(i * chunk, chunk)
            loads[i].wait()
            out_ref[at, :] = low_ref[at, :].astype(F32)
            stores[i].start()
        for store in stores:
            store.wait()

    out = spec((rows, columns), F32)
    return note(pl.pallas_call(
        kernel,
        out_shape=out,
        in_specs=[pl.BlockSpec(memory_space=pltpu.SMEM)]
        + [pl.BlockSpec(memory_space=pl.ANY)] * (len(flat) + len(deps)),
        out_specs=pl.BlockSpec(memory_space=pl.ANY),
        scratch_shapes=[
            pltpu.VMEM(out.shape, BF), pltpu.VMEM(out.shape, F32),
            pltpu.SemaphoreType.DMA((cuts,)), pltpu.SemaphoreType.DMA((cuts,)),
        ],
        compiler_params=pltpu.CompilerParams(vmem_limit_bytes=6 * rows * columns + VMEM_SPARE),
        cost_estimate=LIGHT,
    )(flags, *flat, *deps))


def norm_back(dy, kept, gain):
    hat, inv = kept
    t = dy * gain
    dv = (
        t
        - jnp.mean(t, axis=-1, keepdims=True)
        - hat * jnp.mean(t * hat, axis=-1, keepdims=True)
    ) * inv
    return dv, jnp.stack([jnp.sum(dy * hat, axis=0), jnp.sum(dy, axis=0)])


def on_device(
    layer_in, segments, cotangent, self_qkv, self_out, cross_proj, ffn_up, ffn_down,
    norm_gain, norm_bias,
):
    ORDER.clear()
    STRICT[-1] = True
    sec = lax.axis_index("section")
    n = lax.axis_size("tensor")
    zs = lax.axis_size("dp")
    z = lax.axis_index("dp")
    t = lax.axis_index("tensor")
    tp = n // 2
    bits = tp.bit_length() - 1
    x = t % tp
    fs = t // tp
    micro, share, width = layer_in.shape[1:]
    packed, length = segments.shape[2:]
    rows = packed * length
    assert micro == 4 and zs == 4
    is0 = sec == 0
    gain, bias = norm_gain[0], norm_bias[0]

    def to_core(v, core):
        return lax.ppermute(v, "section", [(1 - core, core)])

    def flip(v, bit, core=None):
        if core is None:
            return lax.ppermute(v, "tensor", [(i, i ^ (1 << bit)) for i in range(n)])
        return lax.ppermute(
            v,
            ("section", "tensor"),
            [(core * n + i, core * n + (i ^ (1 << bit))) for i in range(n)],
        )

    def z_on(v, core, pairs):
        if core is None:
            return lax.ppermute(v, "dp", pairs)
        if core is None:
            return lax.ppermute(v, "dp", pairs)
        if core is None:
            return lax.ppermute(v, "dp", pairs)
        return lax.ppermute(v, ("section", "dp"), [(core * zs + a, core * zs + b) for a, b in pairs])

    def tp_sum(v, core=None):
        for bit in range(bits):
            got = flip(v, bit, core)
            if bit < bits - 1:
                v = (v.astype(F32) + got.astype(F32)).astype(BF)
        return v, got

    def tp_scatter(v, core):
        cur = v.reshape(2, tp, share, width)
        for bit in reversed(range(bits)):
            half = 1 << bit
            bit_on = (x >> bit) & 1
            parts = cur.reshape(2, 2, half, share, width)
            give = lax.dynamic_index_in_dim(parts, 1 - bit_on, 1, keepdims=False)
            keep = lax.dynamic_index_in_dim(parts, bit_on, 1, keepdims=False)
            total = keep.astype(F32) + flip(give, bit, core).astype(F32)
            cur = total.astype(BF)
        return total.reshape(2 * share, width)

    def own_rows(v):
        return lax.dynamic_index_in_dim(
            v.reshape(2, tp, share, v.shape[-1]), x, 1, keepdims=False
        ).reshape(2 * share, v.shape[-1])

    def ordered(is_first, own, other, axis=0):
        first = jnp.where(is_first, own, other)
        second = jnp.where(is_first, other, own)
        return jnp.stack([first, second], axis=axis)

    def gather_micro(keep, got, core=None):
        count = keep.shape[0]
        cur = ordered(fs == 0, keep, got, axis=1)[:, :, None]
        for bit in range(bits):
            got = flip(cur, bit, core)
            cur = ordered((x >> bit) & 1 == 0, cur, got, axis=2).reshape(
                count, 2, 2 << bit, share, width
            )
        return cur.reshape(count, rows, width)

    def scatter_micro(streams):
        blocks = jnp.stack([v.reshape(2, share, width) for v in streams], axis=1)
        keep = lax.dynamic_index_in_dim(blocks, fs, 0, keepdims=False)
        give = lax.dynamic_index_in_dim(blocks, 1 - fs, 0, keepdims=False)
        return ordered(fs == 0, keep, flip(give, bits)).reshape(1, micro, share, width)

    class Reduction:
        def __init__(self, core, own, near):
            self.core, self.value, self.step = core, own, 0
            self.got = None if near is None else flip(near, bits, core)

        def forward(self, value):
            self.value = value
            inward, middle, outward = ((0, 1), (3, 2)), ((1, 2), (2, 1)), ((1, 0), (2, 3))
            self.got = z_on(self.value, self.core, (inward, middle, outward)[self.step])
            self.step += 1
            return self.value

    def z_sum(g, core):
        half = zs // 2
        for k in range(half - 1):
            got = z_on(g, core, [(k, k + 1), (zs - 1 - k, zs - 2 - k)])
            g = (g.astype(F32) + got.astype(F32)).astype(g.dtype)
        got = z_on(g, core, [(half - 1, half), (half, half - 1)])
        g = (g.astype(F32) + got.astype(F32)).astype(g.dtype)
        for k in reversed(range(half - 1)):
            got = z_on(g, core, [(k + 1, k), (zs - 2 - k, zs - 1 - k)])
            g = jnp.where((z == k) | (z == zs - 1 - k), got, g)
        return g

    streams = range(2)
    by_slot = layer_in[0].reshape(2, 2, share, width)
    src_keep = lax.dynamic_index_in_dim(by_slot, fs, 0, keepdims=False)
    src_give = lax.dynamic_index_in_dim(by_slot, 1 - fs, 0, keepdims=False)
    src_got = flip(src_give, bits)
    src = [gather_micro(src_keep[j : j + 1], src_got[j : j + 1])[0] for j in streams]
    segs = lax.dynamic_index_in_dim(
        segments.reshape(2, 2, 2, packed, length), fs, 1, keepdims=False
    )
    seg_e = [segs[0, j] for j in streams]
    seg_d = [segs[1, j] for j in streams]
    seg_own = [jnp.where(is0, e, d) for e, d in zip(seg_e, seg_d)]
    outer = (z == 0) | (z == zs - 1)
    flags = jnp.stack([sec, z % 2, outer]).astype(jnp.int32)

    def fetch(weights, core=None, deps=()):
        if len({w.shape[1] for w in weights}) > 1:
            return [fetch([w], core, deps)[0] for w in weights]
        p = flip(pack_rows(flags, weights, deps), bits, core)
        q = z_on(p, core, [(i, i ^ 1) for i in range(zs)])
        pairs, at = [], 0
        for w in weights:
            pairs.append((w, Near(w.shape, p, q, at)))
            at += w.shape[0] // 2
        return pairs

    STRICT[-1] = False
    (w_qkv,) = fetch([self_qkv[0]])
    (w_out,) = fetch([self_out[0]])
    early = [fetch([w[0]], 0, [src_got])[0] for w in (ffn_up, ffn_down)]
    (w_cross,) = fetch([cross_proj[0]], None, [src[1]])
    late = fetch([ffn_up[0], ffn_down[0]], 1, [src[1]])

    def row(v, i):
        return v[i : i + 1]

    def ln(i):
        return row(gain, i), row(bias, i)

    STRICT[-1] = True
    start, kept_in, sa, keep_s = ([None] * 2 for _ in range(4))
    for j in streams:
        start[j], *kept_in[j], qkv, o, lse, part = self_forward(
            flags, src[j], seg_own[j], *ln(1), w_qkv, w_out
        )
        keep_s[j] = (qkv, o, lse)
        sa[j] = tp_sum(part)
    mid, kept_e1, keep_fe, ff = ([None] * 2 for _ in range(4))
    for j in streams:
        mid[j], *kept_e1[j], hidden, slope, part = ffn_forward(
            0, flags, start[j], sa[j], *ln(0), *early
        )
        keep_fe[j] = (hidden, slope)
        ff[j] = tp_sum(part, 0)
    memory, kept_mem, kv, d1, kept_d1, q, ca, keep_c = ([None] * 2 for _ in range(8))
    for j in streams:
        d1[j], *kept_d1[j], q[j] = norm_project(1, flags, start[j], sa[j], *ln(0), w_cross)
        memory[j], *kept_mem[j], kv[j] = norm_project(0, flags, mid[j], ff[j], *ln(2), w_cross)
        kv[j] = to_core(kv[j], 1)
    cot_by_slot = cotangent.reshape(2, 2, share, width)
    cot_keep = lax.dynamic_index_in_dim(cot_by_slot, fs, 0, keepdims=False)
    cot_give = lax.dynamic_index_in_dim(cot_by_slot, 1 - fs, 0, keepdims=False)
    for j in streams:
        *keep_c[j], part = cross_forward(1, flags, q[j], kv[j], seg_d[j], seg_e[j], w_cross)
        ca[j] = tp_sum(part, 1)
    cot = gather_micro(cot_keep, flip(after(cot_give, keep_c[0][0]), bits, 1), 1)
    d2, kept_d2, keep_fd = ([None] * 2 for _ in range(3))
    for j in streams:
        d2[j], *kept_d2[j], hidden, slope, part = ffn_forward(
            1, flags, d1[j], ca[j], *ln(1), *late
        )
        keep_fd[j] = (hidden, slope)
        ff[j] = tp_sum(part, 1)

    STRICT[-1] = False
    def pick(items, i):
        return [item[i] for item in items]

    def height(group):
        return group[0][0].shape[1] // (2 if group[2] else 1)

    def reduced(enc, dec, cuts=1, sums=()):
        heights = {height(g) for g in (*enc, *dec)}
        widths = {sum(g[1][0].shape[1] // (1 if g[2] else 2) for g in own) for own in (enc, dec) if own}
        if len(heights) > 1 or len(widths) > 1:
            advance((sums, 0))
            return [reduced([g], [], cuts)[0] for g in enc] + [
                reduced([], [g], cuts)[0] for g in dec
            ]
        core = None if enc and dec else 0 if enc else 1
        blocks = weight_grads(flags, (enc, dec), (), cuts, sums)
        chains = [Reduction(core, *pair) for pair in zip(blocks[:cuts], blocks[cuts:])]
        places = []
        for own in (enc, dec):
            at = 0
            for lefts, rights, split_left in own:
                places.append((chains, at))
                at += rights[0].shape[1] // (1 if split_left else 2)
        return places

    def chains_of(places):
        return list({id(chain): chain for place in places for chain in place[0]}.values())

    def advance(*places, deps=()):
        chains = [chain for chain in chains_of(places) if chain.step < 3]
        if chains:
            pairs = [(chain.core, chain.value, chain.got) for chain in chains]
            for chain, value in zip(chains, add_pairs(flags, pairs, deps)):
                chain.forward(value)
        return chains

    def arrived(*places):
        return [chain.got for chain in chains_of(places)]

    def soon(pair):
        return (pair[0], after(pair[1]))

    decoded, df, du, back, n_out, n_d2, n_d1, n_mem, n_e1, n_in = ([None] * 2 for _ in range(10))
    for j in streams:
        decoded[j], df[j], n_out[j], du[j], part = top_backward(
            1, flags, d2[j], ff[j], cot[j], *ln(2), keep_fd[j][1], *late
        )
        back[j] = tp_sum(part, 1)

    dca, dq, dkv, dmem, ds, dqkv, grad_d, grad_e, dfe, due, backe = ([None] * 2 for _ in range(11))
    es, eqkv = ([None] * 2 for _ in range(2))

    def cross_step(j):
        dca[j], n_d2[j], dq[j], grad, part = cross_backward(
            1, flags, (df[j], *back[j]), kept_d2[j], row(gain, 1), q[j], kv[j], seg_d[j], seg_e[j],
            *keep_c[j], w_cross,
        )
        dkv[j] = to_core(grad, 0)
        dmem[j] = tp_sum(memory_backward(0, flags, dkv[j], w_cross), 0)
        back[j] = tp_sum(part, 1)

    def ffn_step(j):
        dfe[j], n_mem[j], due[j], part = ffn_backward(
            0, flags, dmem[j], kept_mem[j], row(gain, 2), keep_fe[j][1], *early,
        )
        backe[j] = tp_sum(part, 0)

    def dec_step(j, sums):
        ds[j], n_d1[j], dqkv[j], part = self_backward(
            1, flags, (dca[j], *back[j]), kept_d1[j], row(gain, 0), *keep_s[j], seg_own[j], w_qkv,
            w_out, sums=sums,
        )
        grad_d[j] = own_rows(ds[j]).astype(F32) + tp_scatter(part, 1)

    def enc_step(j):
        es[j], n_e1[j], eqkv[j], part = self_backward(
            0, flags, (dfe[j], *backe[j]), kept_e1[j], row(gain, 0), *keep_s[j], seg_own[j], w_qkv,
            w_out,
        )
        dy = own_rows(es[j]).astype(F32) + tp_scatter(part, 0)
        hat = own_rows(kept_in[j][0]).astype(F32)
        dv, n_in[j] = norm_back(dy, (hat, own_rows(kept_in[j][1])[:, :1]), gain[1])
        grad_e[j] = dv.astype(BF)

    cross_step(0)
    cross_step(1)
    (gd_down,) = reduced([], [(pick(keep_fd, 0), df, True)])
    ffn_step(0)
    (gd_up,) = reduced([], [(d2, du, False)])
    ffn_step(1)
    dec_step(0, [])
    enc_step(0)
    dec_step(1, gd_down[0])
    ge_cross, ge_down, gd_cross, gd_qkv, gd_out = reduced(
        [(memory, dkv, False), (pick(keep_fe, 0), dfe, True)],
        [
            ((*d1, *dca), (*dq, *pick(keep_c, 0)), False),
            (start, dqkv, False),
            (ds, pick(keep_s, 1), False),
        ],
        2,
    )
    STRICT[-1] = True
    enc_step(1)
    advance(gd_up, gd_down)
    ge_up, ge_qkv, ge_out = reduced(
        [(mid, due, False), (start, eqkv, False), (es, pick(keep_s, 1), False)], [], 2
    )
    layer_out = scatter_micro([own_rows(jnp.where(is0, m, d)) for m, d in zip(memory, decoded)])

    def part(place, i):
        return ([place[0][i % len(place[0])]], 0)

    p1a, p1b = part(ge_cross, 0), part(ge_cross, 1)
    p2a, p2b = part(ge_up, 0), part(ge_up, 1)
    advance(p1a, gd_down, gd_up, deps=[layer_out])

    once = 1.0 / tp
    norms = jnp.where(
        is0,
        jnp.stack([sum(n_e1).sum(1) * once, sum(n_in), sum(n_mem).sum(1) * once], axis=1),
        jnp.stack([sum(n_d1), sum(n_d2), sum(n_out)], axis=1).sum(2) * once,
    )

    def total(enc, dec, columns, turned=False):
        kept, got = (
            [([getattr(chain, name) for chain in chains], at) for chains, at in (enc, dec)]
            for name in ("value", "got")
        )
        if columns % 128 == 0 and enc[1] % 128 == 0 and dec[1] % 128 == 0 and not turned:
            return finish(flags, kept, got, columns)[None]
        kept, got = (
            jnp.where(is0, *(jnp.concatenate(rows)[:, at : at + columns] for rows, at in pair))
            for pair in (kept, got)
        )
        kept = jnp.where(outer, got, kept)
        return (jnp.transpose(kept) if turned else kept).astype(F32)[None]

    def norms_step(norms, bit):
        bit_on = (t >> bit) & 1
        parts = norms.reshape(2, 3, 2, -1)
        return lax.dynamic_index_in_dim(parts, bit_on, 2, keepdims=False) + flip(
            lax.dynamic_index_in_dim(parts, 1 - bit_on, 2, keepdims=False), bit
        )

    for bit in reversed(range(bits + 1)):
        norms = norms_step(norms, bit)
    input_grad = scatter_micro([jnp.where(is0, e, d.astype(BF)) for e, d in zip(grad_e, grad_d)])
    norms_sum = Reduction(None, norms, None)
    advance(p1b, gd_up, p1a, deps=[*arrived(gd_down), input_grad, norms])
    norms_sum.forward(norms)
    advance(p2a, p1b, p1a, deps=[*arrived(gd_up), norms_sum.got])
    norms_sum.forward(norms_sum.value + norms_sum.got)
    advance(p2b, p2a, p1b, deps=[*arrived(p1a), norms_sum.got])
    norms_sum.forward(norms_sum.value + norms_sum.got)
    advance(p2b, p2a, deps=[*arrived(p1b), norms_sum.got])
    advance(p2b, deps=arrived(p2a))
    everything = (
        ge_cross, ge_down, gd_cross, gd_qkv, gd_out, ge_up, ge_qkv, ge_out, gd_down, gd_up
    )
    while advance(*everything):
        pass
    g_cross = total(ge_cross, gd_cross, cross_proj.shape[2])
    g_down = total(ge_down, gd_down, width)
    norms = jnp.where(outer, norms_sum.got, norms_sum.value)
    totals = (
        total(ge_qkv, gd_qkv, self_qkv.shape[2]),
        total(ge_out, gd_out, self_out.shape[1], True),
        g_cross, total(ge_up, gd_up, ffn_up.shape[2]), g_down,
    )
    return (layer_out, input_grad, *totals, norms[0][None], norms[1][None])


def solution(mesh):
    return jax.shard_map(
        on_device,
        mesh=mesh,
        in_specs=(
            P("section", None, ("dp", "tensor"), None),
            P(None, None, "dp", None),
            P(None, ("dp", "tensor"), None),
            P("section", None, "tensor"),
            P("section", "tensor", None),
            P("section", None, "tensor"),
            P("section", None, "tensor"),
            P("section", "tensor", None),
            P("section", None, None),
            P("section", None, None),
        ),
        out_specs=(
            P("section", None, ("dp", "tensor"), None),
            P("section", None, ("dp", "tensor"), None),
            P("section", None, "tensor"),
            P("section", "tensor", None),
            P("section", None, "tensor"),
            P("section", None, "tensor"),
            P("section", "tensor", None),
            P("section", None, "tensor"),
            P("section", None, "tensor"),
        ),
        check_vma=False,
    )
```

```python
import math

import jax
import jax.numpy as jnp
from jax import lax
from jax.experimental import pallas as pl
from jax.experimental.pallas import tpu as pltpu
from jax.sharding import PartitionSpec as P

HD = 64
EPS = 1e-05
MASKED = -1e30
BF = jnp.bfloat16
F32 = jnp.float32
VMEM_SPARE = 6 * 1024 * 1024
GELU_C = 0.7071067811865476
PHI_C = 0.3989422804014327


LIGHT = pl.CostEstimate(flops=1024, bytes_accessed=1024, transcendentals=0)


def mm(a, b):
    return jnp.dot(a, b, preferred_element_type=F32)


def mm_bt(a, b):
    return lax.dot_general(a, b, (((1,), (1,)), ((), ())), preferred_element_type=F32)


def mm_at(a, b):
    return lax.dot_general(a, b, (((0,), (0,)), ((), ())), preferred_element_type=F32)


def spec(shape, dtype=BF):
    return jax.ShapeDtypeStruct(shape, dtype)


class Saved:
    def __init__(self, shape, dtype=BF):
        self.shape, self.dtype, self.size = shape, jnp.dtype(dtype), math.prod(shape)


def in_hbm(array):
    return pltpu.with_memory_space_constraint(array, pltpu.HBM)


class Near:
    def __init__(self, shape, p, q=None, at=0):
        self.shape, self.p, self.q, self.at = shape, p, q, at
        self.dtype, self.size = p.dtype, shape[0] * shape[1]


STRICT = [True]
ORDER = []


def in_order(deps):
    return (*deps, *ORDER[-1:]) if STRICT[-1] else tuple(deps)


def note(results):
    ORDER.append(results[0] if isinstance(results, (tuple, list)) else results)
    return results


def sectioned(
    body, core, flags, small, big, outs, scratch, flops, trans=0, deps=(), owners=None, sums=()
):
    deps = in_order(deps)
    terms = [array for chain in sums for array in (chain.value, chain.got)]
    n_terms = len(terms)
    sources, places = [], []
    for i, array in enumerate(big):
        if isinstance(array, Near) and array.q is None:
            places.append((i, array.shape[0], array.at, None))
            sources.append(array.p)
        elif isinstance(array, Near):
            half = array.shape[0] // 2
            for turn, part in enumerate((array.p, array.q)):
                places.append((i, half, array.at, turn))
                sources.append(part)
        else:
            places.append((i, None, None, None))
            sources.append(array)
    n_small, n_big, n_deps, n_out = len(small), len(big), len(deps), len(outs)
    n_src = len(sources)

    def kernel(flags_ref, *refs):
        small_refs = refs[:n_small]
        big_hbm = refs[n_small : n_small + n_src]
        at = n_small + n_src
        term_hbm = refs[at : at + n_terms]
        at += n_terms + n_deps
        out_hbm = refs[at : at + n_out]
        at += n_out
        sum_hbm = refs[at : at + len(sums)]
        at += len(sums)
        big_refs = refs[at : at + n_big]
        at += n_big
        out_refs = refs[at : at + n_out]
        at += n_out
        term_refs = refs[at : at + n_terms]
        at += n_terms
        extra = refs[at:-4]
        in_sem, out_sem, term_sem, sum_sem = refs[-4:]

        def start_sums():
            loads = [
                pltpu.make_async_copy(term_hbm[i], term_refs[i], term_sem.at[i])
                for i in range(n_terms)
            ]
            for load in loads:
                load.start()
            return loads

        def end_sums(loads):
            stores = []
            for i in range(len(sums)):
                loads[2 * i].wait()
                loads[2 * i + 1].wait()
                a_ref, b_ref = term_refs[2 * i], term_refs[2 * i + 1]
                chunk = 64 if a_ref.shape[0] % 64 == 0 else a_ref.shape[0]

                @pl.loop(0, a_ref.shape[0] // chunk)
                def _(r):
                    at = pl.ds(pl.multiple_of(r * chunk, chunk), chunk)
                    a_ref[at, :] = (a_ref[at, :].astype(F32) + b_ref[at, :].astype(F32)).astype(BF)

                stores.append(pltpu.make_async_copy(a_ref, sum_hbm[i], sum_sem.at[i]))
                stores[-1].start()
            return stores

        def run():
            copies = [[] for _ in range(n_big)]
            for s, (i, half, first, turn) in enumerate(places):
                if half is None:
                    copy = pltpu.make_async_copy(big_hbm[s], big_refs[i], in_sem.at[s])
                elif turn is None:
                    copy = pltpu.make_async_copy(
                        big_hbm[s].at[pl.ds(first, half), :], big_refs[i], in_sem.at[s]
                    )
                else:
                    odd = flags_ref[1] if turn == 0 else 1 - flags_ref[1]
                    copy = pltpu.make_async_copy(
                        big_hbm[s].at[pl.ds(first, half), :],
                        big_refs[i].at[pl.ds(pl.multiple_of(odd * half, half), half), :],
                        in_sem.at[s],
                    )
                if owners is None:
                    copy.start()
                else:
                    pl.when(flags_ref[0] == owners[i])(copy.start)
                copies[i].append(copy)
            done = [
                pltpu.make_async_copy(out_refs[i], out_hbm[i], out_sem.at[i]) for i in range(n_out)
            ]
            loads = start_sums() if sums and core is not None else None
            body(
                flags_ref, small_refs, big_refs, out_refs, extra,
                lambda *which: [copy.wait() for i in which for copy in copies[i]],
                lambda *which: [done[i].start() for i in which],
            )
            if loads:
                done.extend(end_sums(loads))
            for copy in done:
                copy.wait()

        if core is None:
            run()
        else:
            pl.when(flags_ref[0] == core)(run)
        if sums and core is None:

            @pl.when(flags_ref[0] == sums[0].core)
            def _():
                for copy in end_sums(start_sums()):
                    copy.wait()

    nbytes = sum(a.size * a.dtype.itemsize for a in (*big, *outs))
    nbytes += sum(a.size * 2 for a in terms)
    held = nbytes + sum(math.prod(a.shape) * jnp.dtype(a.dtype).itemsize for a in scratch)
    results = note(pl.pallas_call(
        kernel,
        out_shape=tuple(pltpu.HBM(a.shape, a.dtype) if isinstance(a, Saved) else a for a in outs)
        + tuple(spec(chain.value.shape) for chain in sums),
        in_specs=[pl.BlockSpec(memory_space=pltpu.SMEM)]
        + [pl.BlockSpec(memory_space=pltpu.VMEM)] * n_small
        + [pl.BlockSpec(memory_space=pl.ANY)] * (n_src + n_terms + n_deps),
        out_specs=tuple(
            pl.BlockSpec(memory_space=pltpu.HBM if isinstance(a, Saved) else pl.ANY) for a in outs
        )
        + tuple([pl.BlockSpec(memory_space=pl.ANY)] * len(sums)),
        scratch_shapes=[pltpu.VMEM(a.shape, a.dtype) for a in (*big, *outs)]
        + [pltpu.VMEM(a.shape, BF) for a in terms]
        + list(scratch)
        + [
            pltpu.SemaphoreType.DMA((max(1, n_src),)), pltpu.SemaphoreType.DMA((n_out,)),
            pltpu.SemaphoreType.DMA((max(1, n_terms),)),
            pltpu.SemaphoreType.DMA((max(1, len(sums)),)),
        ],
        compiler_params=pltpu.CompilerParams(vmem_limit_bytes=int(held) + VMEM_SPARE),
        cost_estimate=LIGHT,
    )(flags, *small, *sources, *terms, *deps))
    for chain, value in zip(sums, results[n_out:]):
        chain.forward(value)
    return results[:n_out]


def norm_rows(terms, gain, bias, x_ref, hat_ref, inv_ref, chunk=32):
    rows, width = x_ref.shape

    @pl.loop(0, rows // chunk, unroll=4)
    def _(i):
        at = pl.ds(pl.multiple_of(i * chunk, chunk), chunk)
        v = sum(term[at, :].astype(F32) for term in terms)
        centre = v - jnp.mean(v, axis=-1, keepdims=True)
        inv = lax.rsqrt(jnp.mean(centre * centre, axis=-1, keepdims=True) + EPS)
        hat = centre * inv
        x_ref[at, :] = (hat * gain[...] + bias[...]).astype(BF)
        if hat_ref is not None:
            hat_ref[at, :] = hat.astype(BF)
            inv_ref[at, :] = jnp.broadcast_to(inv, (chunk, 128))


def norm_back_rows(terms, hat_ref, inv_ref, gain, dv_ref, n_ref, chunk=32):
    rows, width = dv_ref.shape

    def step(i, sums):
        at = pl.ds(pl.multiple_of(i * chunk, chunk), chunk)
        dy = sum(term[at, :].astype(F32) for term in terms)
        hat = hat_ref[at, :].astype(F32)
        t = dy * gain[...]
        dv = (
            t
            - jnp.mean(t, axis=-1, keepdims=True)
            - hat * jnp.mean(t * hat, axis=-1, keepdims=True)
        ) * inv_ref[at, :1]
        dv_ref[at, :] = dv.astype(BF)
        return (
            sums[0] + (dy * hat).reshape(chunk // 8, 8, width).sum(0),
            sums[1] + dy.reshape(chunk // 8, 8, width).sum(0),
        )

    zero = jnp.zeros((8, width), F32)
    n_ref[0], n_ref[1] = lax.fori_loop(0, rows // chunk, step, (zero, zero), unroll=4)


def matmul_into(x_ref, w_ref, out_ref, at=0, tile=256):
    columns = w_ref.shape[1]
    tile = min(tile, columns)
    for c in range(0, columns, tile):
        out_ref[:, at + c : at + c + tile] = mm(x_ref[...], w_ref[:, c : c + tile]).astype(BF)


def matmul_bt_into(x_ref, w_ref, out_ref, at=0, tile=256):
    rows = w_ref.shape[0]
    tile = min(tile, rows)
    for c in range(0, rows, tile):
        out_ref[:, at + c : at + c + tile] = mm_bt(x_ref[...], w_ref[c : c + tile, :]).astype(BF)


def attend(heads, length, step, offsets, o_step, causal, q_ref, kv_ref, segq, segk, o_ref, lse_ref, bias_ref):
    q_off, k_off, v_off, o_off = offsets
    tile = min(256, length)
    if o_step != HD:
        o_ref[...] = jnp.zeros_like(o_ref)
    lse_ref[...] = jnp.zeros_like(lse_ref)
    for p in range(q_ref.shape[0] // length):
        base = p * length
        all_rows = slice(base, base + length)
        same = segq[all_rows, :] == segk[p : p + 1, :]
        if causal is not None:
            rows = lax.broadcasted_iota(jnp.int32, (length, length), 0)
            cols = lax.broadcasted_iota(jnp.int32, (length, length), 1)
            same = same & (cols * causal <= rows)
        bias_ref[...] = jnp.where(same, 0.0, MASKED)
        for h in range(heads):
            k = kv_ref[all_rows, h * step + k_off : h * step + k_off + HD]
            v = kv_ref[all_rows, h * step + v_off : h * step + v_off + HD]
            for r in range(0, length, tile):
                at = slice(base + r, base + r + tile)
                q = q_ref[at, h * step + q_off : h * step + q_off + HD] * jnp.asarray(HD**-0.5, BF)
                s = mm_bt(q, k) + bias_ref[r : r + tile, :]
                top = jnp.max(s, axis=-1, keepdims=True)
                e = jnp.exp(s - top)
                total = jnp.sum(e, axis=-1, keepdims=True)
                prob = (e * (1.0 / total)).astype(BF)
                o_ref[at, h * o_step + o_off : h * o_step + o_off + HD] = mm(prob, v).astype(BF)
                lse_ref[at, h : h + 1] = top + jnp.log(total)


def attend_back(
    heads, length, step, offsets, o_step, causal, q_ref, kv_ref, segq, segk, o_ref, lse_ref, do_ref,
    dq_ref, dkv_ref, bias_ref, inner_ref,
):
    q_off, k_off, v_off, o_off = offsets
    tile = min(256, length)
    if dq_ref is not dkv_ref:
        dq_ref[...] = jnp.zeros_like(dq_ref)
    for p in range(q_ref.shape[0] // length):
        base = p * length
        all_rows = slice(base, base + length)
        same = segk[all_rows, :] == segq[p : p + 1, :]
        if causal is not None:
            keys = lax.broadcasted_iota(jnp.int32, (length, length), 0)
            queries = lax.broadcasted_iota(jnp.int32, (length, length), 1)
            same = same & (keys * causal <= queries)
        bias_ref[...] = jnp.where(same, 0.0, MASKED)
        inner_ref[...] = jnp.zeros_like(inner_ref)
        for h in range(heads):
            cols = slice(h * o_step + o_off, h * o_step + o_off + HD)
            prod = do_ref[all_rows, cols].astype(F32) * o_ref[all_rows, cols].astype(F32)
            inner_ref[:, h : h + 1] = jnp.sum(prod, axis=-1, keepdims=True)
        inner_t = jnp.transpose(inner_ref[...])
        lse_t = jnp.transpose(lse_ref[all_rows, :])
        for h in range(heads):
            q_cols = slice(h * step + q_off, h * step + q_off + HD)
            k_cols = slice(h * step + k_off, h * step + k_off + HD)
            v_cols = slice(h * step + v_off, h * step + v_off + HD)
            q = q_ref[all_rows, q_cols] * jnp.asarray(HD**-0.5, BF)
            do = do_ref[all_rows, h * o_step + o_off : h * o_step + o_off + HD]
            dq = jnp.zeros((length, HD), F32)
            for r in range(0, length, tile):
                rows = slice(base + r, base + r + tile)
                k = kv_ref[rows, k_cols]
                v = kv_ref[rows, v_cols]
                s = mm_bt(k, q) + bias_ref[r : r + tile, :]
                prob = jnp.exp(s - lse_t[h : h + 1, :])
                dkv_ref[rows, v_cols] = mm(prob.astype(BF), do).astype(BF)
                ds = (prob * (mm_bt(v, do) - inner_t[h : h + 1, :])).astype(BF)
                dkv_ref[rows, k_cols] = mm(ds, q).astype(BF)
                dq = dq + mm_at(ds, k)
            dq_ref[all_rows, q_cols] = (dq * HD**-0.5).astype(BF)


SELF_AT = (0, HD, 2 * HD, 0)
CROSS_AT = (0, 0, HD, HD)


def self_forward(flags, src, seg, gain, bias, w_qkv, w_out, deps=()):
    packed, length = seg.shape
    rows, width = src.shape
    heads = 2 * w_out[0].shape[0] // HD
    part = w_qkv[0].shape[1]

    def body(flags, small, big, outs, extra, wait, flush):
        segq, segk, gain, bias = small
        src, qkv_a, qkv_b, out_a, out_b = big
        x, hat, inv, qkv, o, lse, partial = outs
        (mask,) = extra
        wait(0)

        @pl.when(flags[0] == 0)
        def _():
            norm_rows([src], gain, bias, x, hat, inv)

        @pl.when(flags[0] != 0)
        def _():
            x[...] = src[...]

        flush(0, 1, 2)
        wait(1)
        matmul_into(x, qkv_a, qkv)
        wait(2)
        matmul_into(x, qkv_b, qkv, part)
        flush(3)
        attend(heads, length, 3 * HD, SELF_AT, HD, flags[0], qkv, qkv, segq, segk, o, lse, mask)
        flush(4, 5)
        wait(3, 4)
        half = heads // 2 * HD
        for c in range(0, width, 256):
            partial[:, c : c + 256] = (
                mm(o[:, :half], out_a[:, c : c + 256]) + mm(o[:, half:], out_b[:, c : c + 256])
            ).astype(BF)
        flush(6)

    return sectioned(
        body, None, flags,
        (seg.reshape(rows, 1), seg, gain, bias),
        (src, *w_qkv, *w_out),
        (
            spec((rows, width)), Saved((rows, width)), Saved((rows, 128), F32),
            Saved((rows, 2 * part)), Saved((rows, heads * HD)), Saved((rows, 128), F32),
            spec((rows, width)),
        ),
        [pltpu.VMEM((length, length), F32)],
        2 * rows * width * heads * HD * 4 + 16 * heads * rows * length * HD,
        heads * rows * length, deps,
    )


def ffn_forward(core, flags, res, pair, gain, bias, w_up, w_down, deps=()):
    rows, width = res.shape
    part = w_up[0].shape[1]
    tile = min(512, part)

    def body(flags, small, big, outs, extra, wait, flush):
        gain, bias = small
        res, own, got, up_a, up_b, down_a, down_b = big
        x, hat, inv, hidden, slope, partial = outs
        (total,) = extra
        wait(0, 1, 2)
        norm_rows([res, own, got], gain, bias, x, hat, inv)
        flush(0, 1, 2)
        for i, (up, down) in enumerate(((up_a, down_a), (up_b, down_b))):
            wait(3 + i, 5 + i)
            for c in range(0, part, tile):
                at = slice(i * part + c, i * part + c + tile)
                u = mm(x[...], up[:, c : c + tile])
                phi = 0.5 * (1.0 + lax.erf(u * GELU_C))
                slope[:, at] = (phi + u * (PHI_C * jnp.exp(-0.5 * u * u))).astype(BF)
                hidden[:, at] = (u * phi).astype(BF)
                term = mm(hidden[:, at], down[c : c + tile, :])
                if i == 0 and c == 0:
                    total[...] = term
                else:
                    total[...] += term
        partial[...] = total[...].astype(BF)
        flush(3, 4, 5)

    return sectioned(
        body, core, flags, (gain, bias), (res, *pair, *w_up, *w_down),
        (
            spec((rows, width)), Saved((rows, width)), Saved((rows, 128), F32),
            Saved((rows, 2 * part)), Saved((rows, 2 * part)), spec((rows, width)),
        ),
        [pltpu.VMEM((rows, width), F32)],
        8 * rows * width * part, rows * part * 4, deps,
    )


def norm_project(core, flags, res, pair, gain, bias, w, deps=()):
    rows, width = res.shape
    part = w[0].shape[1]

    def body(flags, small, big, outs, extra, wait, flush):
        gain, bias = small
        res, own, got, w_a, w_b = big
        x, hat, inv, proj = outs
        wait(0, 1, 2)
        norm_rows([res, own, got], gain, bias, x, hat, inv)
        flush(0, 1, 2)
        wait(3)
        matmul_into(x, w_a, proj)
        wait(4)
        matmul_into(x, w_b, proj, part)
        flush(3)

    return sectioned(
        body, core, flags, (gain, bias), (res, *pair, *w),
        (spec((rows, width)), Saved((rows, width)), Saved((rows, 128), F32), spec((rows, 2 * part))),
        [], 4 * rows * width * part, 0, deps,
    )


def cross_forward(core, flags, q, kv, segq, segk, w, deps=()):
    packed, length = segq.shape
    rows = q.shape[0]
    width, part = w[0].shape
    heads = 2 * part // (2 * HD)

    def body(flags, small, big, outs, extra, wait, flush):
        segq, segk = small
        q, kv, w_a, w_b = big
        c, lse, partial = outs
        (mask,) = extra
        wait(0, 1)
        attend(heads, length, 2 * HD, CROSS_AT, 2 * HD, None, q, kv, segq, segk, c, lse, mask)
        flush(0, 1)
        wait(2, 3)
        for r in range(0, width, 256):
            partial[:, r : r + 256] = (
                mm_bt(c[:, :part], w_a[r : r + 256, :]) + mm_bt(c[:, part:], w_b[r : r + 256, :])
            ).astype(BF)
        flush(2)

    return sectioned(
        body, core, flags, (segq.reshape(rows, 1), segk), (q, kv, *w),
        (Saved((rows, 2 * part)), Saved((rows, 128), F32), spec((rows, width))),
        [pltpu.VMEM((length, length), F32)],
        4 * rows * width * part + 16 * heads * rows * length * HD, heads * rows * length, deps,
    )


def ffn_back_loop(df, slope, up, down, du, total, partial, wait, first):
    part = up[0].shape[1]
    tile = min(512, part)
    for i in range(2):
        wait(first + i, first + 2 + i)
        for c in range(0, part, tile):
            at = slice(i * part + c, i * part + c + tile)
            dh = mm_bt(df[...], down[i][c : c + tile, :])
            du[:, at] = (dh * slope[:, at].astype(F32)).astype(BF)
            term = mm_bt(du[:, at], up[i][:, c : c + tile])
            if i == 0 and c == 0:
                total[...] = term
            else:
                total[...] += term
    partial[...] = total[...].astype(BF)


def top_backward(core, flags, res, pair, cot, gain, bias, slope, w_up, w_down, deps=()):
    rows, width = res.shape
    part = w_up[0].shape[1]

    def body(flags, small, big, outs, extra, wait, flush):
        gain, bias = small
        res, own, got, cot, slope, up_a, up_b, down_a, down_b = big
        y, df, n, du, partial = outs
        total, hat, inv = extra
        wait(0, 1, 2)
        norm_rows([res, own, got], gain, bias, y, hat, inv)
        flush(0)
        wait(3)
        norm_back_rows([cot], hat, inv, gain, df, n)
        flush(1, 2)
        wait(4)
        ffn_back_loop(df, slope, (up_a, up_b), (down_a, down_b), du, total, partial, wait, 5)
        flush(3, 4)

    return sectioned(
        body, core, flags, (gain, bias), (res, *pair, in_hbm(cot), in_hbm(slope), *w_up, *w_down),
        (
            Saved((rows, width)), spec((rows, width)), Saved((2, 8, width), F32),
            Saved((rows, 2 * part)), spec((rows, width)),
        ),
        [pltpu.VMEM((rows, width), F32), pltpu.VMEM((rows, width), BF), pltpu.VMEM((rows, 128), F32)],
        8 * rows * width * part, 0, deps,
    )


def ffn_backward(core, flags, terms, kept, gain, slope, w_up, w_down, deps=()):
    rows, width = terms[0].shape
    part = w_up[0].shape[1]
    k = len(terms)

    def body(flags, small, big, outs, extra, wait, flush):
        (gain,) = small
        terms = big[:k]
        hat, inv, slope, up_a, up_b, down_a, down_b = big[k:]
        df, n, du, partial = outs
        (total,) = extra
        wait(*range(k + 2))
        norm_back_rows(terms, hat, inv, gain, df, n)
        flush(0, 1)
        wait(k + 2)
        ffn_back_loop(df, slope, (up_a, up_b), (down_a, down_b), du, total, partial, wait, k + 3)
        flush(2, 3)

    return sectioned(
        body, core, flags, (gain,), (*terms, *map(in_hbm, kept), in_hbm(slope), *w_up, *w_down),
        (
            spec((rows, width)), Saved((2, 8, width), F32), Saved((rows, 2 * part)),
            spec((rows, width)),
        ),
        [pltpu.VMEM((rows, width), F32)],
        8 * rows * width * part, 0, deps,
    )


def cross_backward(core, flags, terms, kept, gain, q, kv, segq, segk, c, lse, w, deps=()):
    packed, length = segq.shape
    rows, width = terms[0].shape
    part = w[0].shape[1]
    heads = 2 * part // (2 * HD)
    k = len(terms)

    def body(flags, small, big, outs, extra, wait, flush):
        segq, segk, gain = small
        terms = big[:k]
        hat, inv, w_a, w_b, q, kv, c, lse = big[k:]
        dca, n, dq, dkv, partial = outs
        dc, mask, inner = extra
        wait(*range(k + 2))
        norm_back_rows(terms, hat, inv, gain, dca, n)
        flush(0, 1)
        wait(k + 2, k + 3)
        matmul_into(dca, w_a, dc)
        matmul_into(dca, w_b, dc, part)
        wait(*range(k + 4, k + 8))
        attend_back(
            heads, length, 2 * HD, CROSS_AT, 2 * HD, None, q, kv, segq, segk, c, lse, dc, dq, dkv,
            mask, inner,
        )
        flush(2, 3)
        for r in range(0, width, 256):
            partial[:, r : r + 256] = (
                mm_bt(dq[:, :part], w_a[r : r + 256, :]) + mm_bt(dq[:, part:], w_b[r : r + 256, :])
            ).astype(BF)
        flush(4)

    return sectioned(
        body, core, flags, (segq, segk.reshape(rows, 1), gain),
        (*terms, *map(in_hbm, kept), *w, *map(in_hbm, (q, kv, c, lse))),
        (
            spec((rows, width)), Saved((2, 8, width), F32), Saved((rows, 2 * part)),
            spec((rows, 2 * part)), spec((rows, width)),
        ),
        [
            pltpu.VMEM((rows, 2 * part), BF), pltpu.VMEM((length, length), F32),
            pltpu.VMEM((length, 128), F32),
        ],
        8 * rows * width * part + 40 * heads * rows * length * HD, heads * rows * length, deps,
    )


def memory_backward(core, flags, dkv, w, deps=()):
    rows = dkv.shape[0]
    width, part = w[0].shape

    def body(flags, small, big, outs, extra, wait, flush):
        dkv, w_a, w_b = big
        (partial,) = outs
        wait(0, 1, 2)
        for r in range(0, width, 256):
            partial[:, r : r + 256] = (
                mm_bt(dkv[:, :part], w_a[r : r + 256, :]) + mm_bt(dkv[:, part:], w_b[r : r + 256, :])
            ).astype(BF)
        flush(0)

    return sectioned(
        body, core, flags, (), (dkv, *w), (spec((rows, width)),), [], 4 * rows * width * part, 0, deps
    )[0]


def self_backward(
    core, flags, terms, kept, gain, qkv, o, lse, seg, w_qkv, w_out, deps=(), sums=()
):
    packed, length = seg.shape
    rows, width = terms[0].shape
    heads = 2 * w_out[0].shape[0] // HD
    part = w_qkv[0].shape[1]
    k = len(terms)

    def body(flags, small, big, outs, extra, wait, flush):
        segq, segk, gain = small
        terms = big[:k]
        hat, inv, out_a, out_b, qkv, o, lse, qkv_a, qkv_b = big[k:]
        ds, n, dqkv, partial = outs
        do, mask, inner = extra
        wait(*range(k + 2))
        norm_back_rows(terms, hat, inv, gain, ds, n)
        flush(0, 1)
        wait(k + 2, k + 3)
        half = heads // 2 * HD
        matmul_bt_into(ds, out_a, do)
        matmul_bt_into(ds, out_b, do, half)
        wait(*range(k + 4, k + 7))
        attend_back(
            heads, length, 3 * HD, SELF_AT, HD, flags[0], qkv, qkv, segq, segk, o, lse, do, dqkv,
            dqkv, mask, inner,
        )
        flush(2)
        wait(k + 7, k + 8)
        for r in range(0, width, 256):
            partial[:, r : r + 256] = (
                mm_bt(dqkv[:, :part], qkv_a[r : r + 256, :])
                + mm_bt(dqkv[:, part:], qkv_b[r : r + 256, :])
            ).astype(BF)
        flush(3)

    return sectioned(
        body, core, flags, (seg, seg.reshape(rows, 1), gain),
        (*terms, *map(in_hbm, kept), *w_out, *map(in_hbm, (qkv, o, lse)), *w_qkv),
        (
            spec((rows, width)), Saved((2, 8, width), F32), Saved((rows, 2 * part)),
            spec((rows, width)),
        ),
        [
            pltpu.VMEM((rows, heads * HD), BF), pltpu.VMEM((length, length), F32),
            pltpu.VMEM((length, 128), F32),
        ],
        2 * rows * width * heads * HD * 4 + 40 * heads * rows * length * HD,
        heads * rows * length, deps, sums=sums,
    )


def weight_grads(flags, groups, deps=(), cuts=1, sums=()):
    lists = [
        in_hbm(array) for own in groups for lefts, rights, _ in own for array in (*lefts, *rights)
    ]
    live = [core for core in range(2) if groups[core]]
    some = groups[live[0]]
    height = some[0][0][0].shape[1] // (2 if some[0][2] else 1)
    widths = [
        [rights[0].shape[1] // (1 if split_left else 2) for _, rights, split_left in own]
        for own in groups
    ]
    piece = height // cuts
    counts = [sum(2 * len(lefts) for lefts, _, _ in own) for own in groups]

    def body(flags, small, big, outs, extra, wait, flush):
        def run(core):
            for i in reversed(range(2)):
                first, at = counts[0] * core, 0
                for g, (lefts, rights, split_left) in enumerate(groups[core]):
                    k = len(lefts)
                    if i == 1:
                        wait(*range(first, first + 2 * k))
                    i_m = i * height if split_left else 0
                    n = widths[core][g]
                    i_n = 0 if split_left else i * n
                    tile = min(256, piece)
                    for r in range(0, height, tile):
                        low = r % piece
                        outs[i * cuts + r // piece][low : low + tile, at : at + n] = sum(
                            mm_at(
                                big[first + j][:, i_m + r : i_m + r + tile],
                                big[first + k + j][:, i_n : i_n + n],
                            )
                            for j in range(k)
                        ).astype(BF)
                    first += 2 * k
                    at += n
                flush(*range(i * cuts, (i + 1) * cuts))

        if len(live) == 1:
            run(live[0])
        else:
            for core in live:
                pl.when(flags[0] == core)(lambda core=core: run(core))

    blocks = tuple(spec((piece, sum(widths[live[0]]))) for _ in range(2 * cuts))
    owners = [0] * counts[0] + [1] * counts[1]
    return sectioned(
        body, live[0] if len(live) == 1 else None, flags, (), lists, blocks, [], 0, 0, deps, owners,
        sums,
    )


def after(array, *deps):
    deps = in_order(deps)
    return note(pl.pallas_call(
        lambda *refs: None,
        out_shape=spec(array.shape, array.dtype),
        in_specs=[pl.BlockSpec(memory_space=pl.ANY)] * (1 + len(deps)),
        out_specs=pl.BlockSpec(memory_space=pl.ANY),
        input_output_aliases={0: 0},
        cost_estimate=LIGHT,
    )(array, *deps))


def pack_rows(flags, weights, deps=(), whole=False):
    deps = in_order(deps)
    halves = [w.shape[0] // (1 if whole else 2) for w in weights]
    out = spec((sum(halves), weights[0].shape[1]))

    def kernel(flags_ref, *refs):
        target, sem = refs[-2:]
        copies, at = [], 0
        for i, half in enumerate(halves):
            first = 0 if whole else pl.multiple_of(flags_ref[1] * half, half)
            copies.append(
                pltpu.make_async_copy(
                    refs[i].at[pl.ds(first, half), :], target.at[pl.ds(at, half), :], sem.at[i]
                )
            )
            at += half
        for copy in copies:
            copy.start()
        for copy in copies:
            copy.wait()

    return note(pl.pallas_call(
        kernel,
        out_shape=out,
        in_specs=[pl.BlockSpec(memory_space=pltpu.SMEM)]
        + [pl.BlockSpec(memory_space=pl.ANY)] * (len(weights) + len(deps)),
        out_specs=pl.BlockSpec(memory_space=pltpu.VMEM),
        scratch_shapes=[pltpu.SemaphoreType.DMA((len(weights),))],
        cost_estimate=LIGHT,
    )(flags, *weights, *deps))


def add_pairs(flags, pairs, deps=()):
    deps = in_order(deps)
    k = len(pairs)
    cuts = [4 if a.shape[0] % 64 == 0 else 1 for _, a, _ in pairs]

    def kernel(flags_ref, *refs):
        terms = refs[: 2 * k]
        outs = refs[2 * k + len(deps) : 3 * k + len(deps)]
        held = refs[3 * k + len(deps) : -2]
        in_sem, out_sem = refs[-2:]
        jobs = []
        for p, (core, a, _) in enumerate(pairs):
            live = flags_ref[0] >= 0 if core is None else flags_ref[0] == core
            chunk = a.shape[0] // cuts[p]
            for i in range(cuts[p]):
                at = pl.ds(i * chunk, chunk)
                loads = [
                    pltpu.make_async_copy(
                        terms[2 * p + j].at[at, :], held[2 * p + j].at[at, :], in_sem.at[2 * p + j, i]
                    )
                    for j in range(2)
                ]
                store = pltpu.make_async_copy(held[2 * p].at[at, :], outs[p].at[at, :], out_sem.at[p, i])
                jobs.append((live, at, held[2 * p], held[2 * p + 1], loads, store))
        for live, _, _, _, loads, _ in jobs:

            @pl.when(live)
            def _():
                for load in loads:
                    load.start()

        for live, at, a_ref, b_ref, loads, store in jobs:

            @pl.when(live)
            def _():
                for load in loads:
                    load.wait()
                a_ref[at, :] = (a_ref[at, :].astype(F32) + b_ref[at, :].astype(F32)).astype(BF)
                store.start()

        for live, _, _, _, _, store in jobs:
            pl.when(live)(store.wait)

    arrays = [array for _, a, b in pairs for array in (a, b)]
    return note(pl.pallas_call(
        kernel,
        out_shape=tuple(spec(a.shape) for _, a, _ in pairs),
        in_specs=[pl.BlockSpec(memory_space=pltpu.SMEM)]
        + [pl.BlockSpec(memory_space=pl.ANY)] * (2 * k + len(deps)),
        out_specs=tuple([pl.BlockSpec(memory_space=pl.ANY)] * k),
        scratch_shapes=[pltpu.VMEM(array.shape, BF) for array in arrays]
        + [pltpu.SemaphoreType.DMA((2 * k, 4)), pltpu.SemaphoreType.DMA((k, 4))],
        compiler_params=pltpu.CompilerParams(
            vmem_limit_bytes=sum(2 * array.size for array in arrays) + VMEM_SPARE
        ),
        cost_estimate=LIGHT,
    )(flags, *arrays, *deps))


def finish(flags, kept, got, columns, deps=()):
    deps = in_order(deps)
    sources = [kept[0], kept[1], got[0], got[1]]
    rows = sum(piece.shape[0] for piece in sources[0][0])
    cuts = 4 if rows % 64 == 0 else max(len(pieces) for pieces, _ in sources)
    chunk = rows // cuts
    flat = [piece for pieces, _ in sources for piece in pieces]

    def kernel(flags_ref, *refs):
        out_hbm, low_ref, out_ref, in_sem, out_sem = refs[len(flat) + len(deps) :]
        loads, stores = [], []
        for i in range(cuts):
            at = pl.ds(i * chunk, chunk)
            first_ref = 0
            for c, (pieces, first) in enumerate(sources):
                size = rows // len(pieces)
                load = pltpu.make_async_copy(
                    refs[first_ref + i * chunk // size].at[
                        pl.ds(i * chunk % size, chunk), pl.ds(first, columns)
                    ],
                    low_ref.at[at, :],
                    in_sem.at[i],
                )
                pl.when(flags_ref[0] + 2 * flags_ref[2] == c)(load.start)
                first_ref += len(pieces)
            loads.append(load)
            stores.append(pltpu.make_async_copy(out_ref.at[at, :], out_hbm.at[at, :], out_sem.at[i]))
        for i in range(cuts):
            at = pl.ds(i * chunk, chunk)
            loads[i].wait()
            out_ref[at, :] = low_ref[at, :].astype(F32)
            stores[i].start()
        for store in stores:
            store.wait()

    out = spec((rows, columns), F32)
    return note(pl.pallas_call(
        kernel,
        out_shape=out,
        in_specs=[pl.BlockSpec(memory_space=pltpu.SMEM)]
        + [pl.BlockSpec(memory_space=pl.ANY)] * (len(flat) + len(deps)),
        out_specs=pl.BlockSpec(memory_space=pl.ANY),
        scratch_shapes=[
            pltpu.VMEM(out.shape, BF), pltpu.VMEM(out.shape, F32),
            pltpu.SemaphoreType.DMA((cuts,)), pltpu.SemaphoreType.DMA((cuts,)),
        ],
        compiler_params=pltpu.CompilerParams(vmem_limit_bytes=6 * rows * columns + VMEM_SPARE),
        cost_estimate=LIGHT,
    )(flags, *flat, *deps))


def norm_back(dy, kept, gain):
    hat, inv = kept
    t = dy * gain
    dv = (
        t
        - jnp.mean(t, axis=-1, keepdims=True)
        - hat * jnp.mean(t * hat, axis=-1, keepdims=True)
    ) * inv
    return dv, jnp.stack([jnp.sum(dy * hat, axis=0), jnp.sum(dy, axis=0)])


def on_device(
    layer_in, segments, cotangent, self_qkv, self_out, cross_proj, ffn_up, ffn_down,
    norm_gain, norm_bias,
):
    ORDER.clear()
    STRICT[-1] = True
    sec = lax.axis_index("section")
    n = lax.axis_size("tensor")
    zs = lax.axis_size("dp")
    z = lax.axis_index("dp")
    t = lax.axis_index("tensor")
    tp = n // 2
    bits = tp.bit_length() - 1
    x = t % tp
    fs = t // tp
    micro, share, width = layer_in.shape[1:]
    packed, length = segments.shape[2:]
    rows = packed * length
    assert micro == 4 and zs == 4
    is0 = sec == 0
    gain, bias = norm_gain[0], norm_bias[0]

    def to_core(v, core):
        return lax.ppermute(v, "section", [(1 - core, core)])

    def flip(v, bit, core=None):
        if core is None:
            return lax.ppermute(v, "tensor", [(i, i ^ (1 << bit)) for i in range(n)])
        return lax.ppermute(
            v,
            ("section", "tensor"),
            [(core * n + i, core * n + (i ^ (1 << bit))) for i in range(n)],
        )

    def z_on(v, core, pairs):
        if core is None:
            return lax.ppermute(v, "dp", pairs)
        if core is None:
            return lax.ppermute(v, "dp", pairs)
        if core is None:
            return lax.ppermute(v, "dp", pairs)
        return lax.ppermute(v, ("section", "dp"), [(core * zs + a, core * zs + b) for a, b in pairs])

    def tp_sum(v, core=None):
        for bit in range(bits):
            got = flip(v, bit, core)
            if bit < bits - 1:
                v = (v.astype(F32) + got.astype(F32)).astype(BF)
        return v, got

    def tp_scatter(v, core):
        cur = v.reshape(2, tp, share, width)
        for bit in reversed(range(bits)):
            half = 1 << bit
            bit_on = (x >> bit) & 1
            parts = cur.reshape(2, 2, half, share, width)
            give = lax.dynamic_index_in_dim(parts, 1 - bit_on, 1, keepdims=False)
            keep = lax.dynamic_index_in_dim(parts, bit_on, 1, keepdims=False)
            total = keep.astype(F32) + flip(give, bit, core).astype(F32)
            cur = total.astype(BF)
        return total.reshape(2 * share, width)

    def own_rows(v):
        return lax.dynamic_index_in_dim(
            v.reshape(2, tp, share, v.shape[-1]), x, 1, keepdims=False
        ).reshape(2 * share, v.shape[-1])

    def ordered(is_first, own, other, axis=0):
        first = jnp.where(is_first, own, other)
        second = jnp.where(is_first, other, own)
        return jnp.stack([first, second], axis=axis)

    def gather_micro(keep, got, core=None):
        count = keep.shape[0]
        cur = ordered(fs == 0, keep, got, axis=1)[:, :, None]
        for bit in range(bits):
            got = flip(cur, bit, core)
            cur = ordered((x >> bit) & 1 == 0, cur, got, axis=2).reshape(
                count, 2, 2 << bit, share, width
            )
        return cur.reshape(count, rows, width)

    def scatter_micro(streams):
        blocks = jnp.stack([v.reshape(2, share, width) for v in streams], axis=1)
        keep = lax.dynamic_index_in_dim(blocks, fs, 0, keepdims=False)
        give = lax.dynamic_index_in_dim(blocks, 1 - fs, 0, keepdims=False)
        return ordered(fs == 0, keep, flip(give, bits)).reshape(1, micro, share, width)

    class Reduction:
        def __init__(self, core, own, near):
            self.core, self.value, self.step = core, own, 0
            self.got = None if near is None else flip(near, bits, core)

        def forward(self, value):
            self.value = value
            inward, middle, outward = ((0, 1), (3, 2)), ((1, 2), (2, 1)), ((1, 0), (2, 3))
            self.got = z_on(self.value, self.core, (inward, middle, outward)[self.step])
            self.step += 1
            return self.value

    def z_sum(g, core):
        half = zs // 2
        for k in range(half - 1):
            got = z_on(g, core, [(k, k + 1), (zs - 1 - k, zs - 2 - k)])
            g = (g.astype(F32) + got.astype(F32)).astype(g.dtype)
        got = z_on(g, core, [(half - 1, half), (half, half - 1)])
        g = (g.astype(F32) + got.astype(F32)).astype(g.dtype)
        for k in reversed(range(half - 1)):
            got = z_on(g, core, [(k + 1, k), (zs - 2 - k, zs - 1 - k)])
            g = jnp.where((z == k) | (z == zs - 1 - k), got, g)
        return g

    streams = range(2)
    by_slot = layer_in[0].reshape(2, 2, share, width)
    src_keep = lax.dynamic_index_in_dim(by_slot, fs, 0, keepdims=False)
    src_give = lax.dynamic_index_in_dim(by_slot, 1 - fs, 0, keepdims=False)
    src_got = flip(src_give, bits)
    src = [gather_micro(src_keep[j : j + 1], src_got[j : j + 1])[0] for j in streams]
    segs = lax.dynamic_index_in_dim(
        segments.reshape(2, 2, 2, packed, length), fs, 1, keepdims=False
    )
    seg_e = [segs[0, j] for j in streams]
    seg_d = [segs[1, j] for j in streams]
    seg_own = [jnp.where(is0, e, d) for e, d in zip(seg_e, seg_d)]
    outer = (z == 0) | (z == zs - 1)
    flags = jnp.stack([sec, z % 2, outer]).astype(jnp.int32)

    def fetch(weights, core=None, deps=()):
        if len({w.shape[1] for w in weights}) > 1:
            return [fetch([w], core, deps)[0] for w in weights]
        p = flip(pack_rows(flags, weights, deps), bits, core)
        q = z_on(p, core, [(i, i ^ 1) for i in range(zs)])
        pairs, at = [], 0
        for w in weights:
            pairs.append((w, Near(w.shape, p, q, at)))
            at += w.shape[0] // 2
        return pairs

    STRICT[-1] = False
    (w_qkv,) = fetch([self_qkv[0]])
    (w_out,) = fetch([self_out[0]])
    early = [fetch([w[0]], 0, [src_got])[0] for w in (ffn_up, ffn_down)]
    (w_cross,) = fetch([cross_proj[0]], None, [src[1]])
    late = fetch([ffn_up[0], ffn_down[0]], 1, [src[1]])

    def row(v, i):
        return v[i : i + 1]

    def ln(i):
        return row(gain, i), row(bias, i)

    STRICT[-1] = True
    start, kept_in, sa, keep_s = ([None] * 2 for _ in range(4))
    for j in streams:
        start[j], *kept_in[j], qkv, o, lse, part = self_forward(
            flags, src[j], seg_own[j], *ln(1), w_qkv, w_out
        )
        keep_s[j] = (qkv, o, lse)
        sa[j] = tp_sum(part)
    mid, kept_e1, keep_fe, ff = ([None] * 2 for _ in range(4))
    for j in streams:
        mid[j], *kept_e1[j], hidden, slope, part = ffn_forward(
            0, flags, start[j], sa[j], *ln(0), *early
        )
        keep_fe[j] = (hidden, slope)
        ff[j] = tp_sum(part, 0)
    memory, kept_mem, kv, d1, kept_d1, q, ca, keep_c = ([None] * 2 for _ in range(8))
    for j in streams:
        d1[j], *kept_d1[j], q[j] = norm_project(1, flags, start[j], sa[j], *ln(0), w_cross)
        memory[j], *kept_mem[j], kv[j] = norm_project(0, flags, mid[j], ff[j], *ln(2), w_cross)
        kv[j] = to_core(kv[j], 1)
    cot_by_slot = cotangent.reshape(2, 2, share, width)
    cot_keep = lax.dynamic_index_in_dim(cot_by_slot, fs, 0, keepdims=False)
    cot_give = lax.dynamic_index_in_dim(cot_by_slot, 1 - fs, 0, keepdims=False)
    for j in streams:
        *keep_c[j], part = cross_forward(1, flags, q[j], kv[j], seg_d[j], seg_e[j], w_cross)
        ca[j] = tp_sum(part, 1)
    cot = gather_micro(cot_keep, flip(after(cot_give, keep_c[0][0]), bits, 1), 1)
    d2, kept_d2, keep_fd = ([None] * 2 for _ in range(3))
    for j in streams:
        d2[j], *kept_d2[j], hidden, slope, part = ffn_forward(
            1, flags, d1[j], ca[j], *ln(1), *late
        )
        keep_fd[j] = (hidden, slope)
        ff[j] = tp_sum(part, 1)

    STRICT[-1] = False
    def pick(items, i):
        return [item[i] for item in items]

    def height(group):
        return group[0][0].shape[1] // (2 if group[2] else 1)

    def reduced(enc, dec, cuts=1, sums=()):
        heights = {height(g) for g in (*enc, *dec)}
        widths = {sum(g[1][0].shape[1] // (1 if g[2] else 2) for g in own) for own in (enc, dec) if own}
        if len(heights) > 1 or len(widths) > 1:
            advance((sums, 0))
            return [reduced([g], [], cuts)[0] for g in enc] + [
                reduced([], [g], cuts)[0] for g in dec
            ]
        core = None if enc and dec else 0 if enc else 1
        blocks = weight_grads(flags, (enc, dec), (), cuts, sums)
        chains = [Reduction(core, *pair) for pair in zip(blocks[:cuts], blocks[cuts:])]
        places = []
        for own in (enc, dec):
            at = 0
            for lefts, rights, split_left in own:
                places.append((chains, at))
                at += rights[0].shape[1] // (1 if split_left else 2)
        return places

    def chains_of(places):
        return list({id(chain): chain for place in places for chain in place[0]}.values())

    def advance(*places, deps=()):
        chains = [chain for chain in chains_of(places) if chain.step < 3]
        if chains:
            pairs = [(chain.core, chain.value, chain.got) for chain in chains]
            for chain, value in zip(chains, add_pairs(flags, pairs, deps)):
                chain.forward(value)
        return chains

    def arrived(*places):
        return [chain.got for chain in chains_of(places)]

    def soon(pair):
        return (pair[0], after(pair[1]))

    decoded, df, du, back, n_out, n_d2, n_d1, n_mem, n_e1, n_in = ([None] * 2 for _ in range(10))
    for j in streams:
        decoded[j], df[j], n_out[j], du[j], part = top_backward(
            1, flags, d2[j], ff[j], cot[j], *ln(2), keep_fd[j][1], *late
        )
        back[j] = tp_sum(part, 1)

    dca, dq, dkv, dmem, ds, dqkv, grad_d, grad_e, dfe, due, backe = ([None] * 2 for _ in range(11))
    es, eqkv = ([None] * 2 for _ in range(2))

    def cross_step(j):
        dca[j], n_d2[j], dq[j], grad, part = cross_backward(
            1, flags, (df[j], *back[j]), kept_d2[j], row(gain, 1), q[j], kv[j], seg_d[j], seg_e[j],
            *keep_c[j], w_cross,
        )
        dkv[j] = to_core(grad, 0)
        dmem[j] = tp_sum(memory_backward(0, flags, dkv[j], w_cross), 0)
        back[j] = tp_sum(part, 1)

    def ffn_step(j):
        dfe[j], n_mem[j], due[j], part = ffn_backward(
            0, flags, dmem[j], kept_mem[j], row(gain, 2), keep_fe[j][1], *early,
        )
        backe[j] = tp_sum(part, 0)

    def dec_step(j, sums):
        ds[j], n_d1[j], dqkv[j], part = self_backward(
            1, flags, (dca[j], *back[j]), kept_d1[j], row(gain, 0), *keep_s[j], seg_own[j], w_qkv,
            w_out, sums=sums,
        )
        grad_d[j] = own_rows(ds[j]).astype(F32) + tp_scatter(part, 1)

    def enc_step(j):
        es[j], n_e1[j], eqkv[j], part = self_backward(
            0, flags, (dfe[j], *backe[j]), kept_e1[j], row(gain, 0), *keep_s[j], seg_own[j], w_qkv,
            w_out,
        )
        dy = own_rows(es[j]).astype(F32) + tp_scatter(part, 0)
        hat = own_rows(kept_in[j][0]).astype(F32)
        dv, n_in[j] = norm_back(dy, (hat, own_rows(kept_in[j][1])[:, :1]), gain[1])
        grad_e[j] = dv.astype(BF)

    cross_step(0)
    cross_step(1)
    (gd_down,) = reduced([], [(pick(keep_fd, 0), df, True)])
    ffn_step(0)
    (gd_up,) = reduced([], [(d2, du, False)])
    ffn_step(1)
    dec_step(0, gd_down[0])
    enc_step(0)
    dec_step(1, gd_down[0] + gd_up[0])
    ge_cross, ge_down, gd_cross, gd_qkv, gd_out = reduced(
        [(memory, dkv, False), (pick(keep_fe, 0), dfe, True)],
        [
            ((*d1, *dca), (*dq, *pick(keep_c, 0)), False),
            (start, dqkv, False),
            (ds, pick(keep_s, 1), False),
        ],
        2,
    )
    STRICT[-1] = True
    enc_step(1)
    advance(gd_up, gd_down)
    ge_up, ge_qkv, ge_out = reduced(
        [(mid, due, False), (start, eqkv, False), (es, pick(keep_s, 1), False)], [], 2
    )
    layer_out = scatter_micro([own_rows(jnp.where(is0, m, d)) for m, d in zip(memory, decoded)])

    def part(place, i):
        return ([place[0][i % len(place[0])]], 0)

    p1a, p1b = part(ge_cross, 0), part(ge_cross, 1)
    p2a, p2b = part(ge_up, 0), part(ge_up, 1)
    advance(p1a, gd_down, gd_up, deps=[layer_out])

    once = 1.0 / tp
    norms = jnp.where(
        is0,
        jnp.stack([sum(n_e1).sum(1) * once, sum(n_in), sum(n_mem).sum(1) * once], axis=1),
        jnp.stack([sum(n_d1), sum(n_d2), sum(n_out)], axis=1).sum(2) * once,
    )

    def total(enc, dec, columns, turned=False):
        kept, got = (
            [([getattr(chain, name) for chain in chains], at) for chains, at in (enc, dec)]
            for name in ("value", "got")
        )
        if columns % 128 == 0 and enc[1] % 128 == 0 and dec[1] % 128 == 0 and not turned:
            return finish(flags, kept, got, columns)[None]
        kept, got = (
            jnp.where(is0, *(jnp.concatenate(rows)[:, at : at + columns] for rows, at in pair))
            for pair in (kept, got)
        )
        kept = jnp.where(outer, got, kept)
        return (jnp.transpose(kept) if turned else kept).astype(F32)[None]

    def norms_step(norms, bit):
        bit_on = (t >> bit) & 1
        parts = norms.reshape(2, 3, 2, -1)
        return lax.dynamic_index_in_dim(parts, bit_on, 2, keepdims=False) + flip(
            lax.dynamic_index_in_dim(parts, 1 - bit_on, 2, keepdims=False), bit
        )

    hops = reversed(range(bits + 1))
    norms = norms_step(norms, next(hops))
    input_grad = scatter_micro([jnp.where(is0, e, d.astype(BF)) for e, d in zip(grad_e, grad_d)])
    advance(p1b, gd_up, p1a, deps=[*arrived(gd_down), norms])
    for bit in hops:
        norms = norms_step(norms, bit)
    norms_sum = Reduction(None, norms, None)
    advance(p2a, p1b, p1a, deps=[*arrived(gd_up), norms, input_grad])
    norms_sum.forward(norms)
    advance(p2b, p2a, p1b, deps=[*arrived(p1a), norms_sum.got])
    norms_sum.forward(norms_sum.value + norms_sum.got)
    advance(p2b, p2a, deps=[*arrived(p1b), norms_sum.got])
    norms_sum.forward(norms_sum.value + norms_sum.got)
    advance(p2b, deps=[*arrived(p2a), norms_sum.got])
    everything = (
        ge_cross, ge_down, gd_cross, gd_qkv, gd_out, ge_up, ge_qkv, ge_out, gd_down, gd_up
    )
    while advance(*everything):
        pass
    g_cross = total(ge_cross, gd_cross, cross_proj.shape[2])
    g_down = total(ge_down, gd_down, width)
    norms = jnp.where(outer, norms_sum.got, norms_sum.value)
    totals = (
        total(ge_qkv, gd_qkv, self_qkv.shape[2]),
        total(ge_out, gd_out, self_out.shape[1], True),
        g_cross, total(ge_up, gd_up, ffn_up.shape[2]), g_down,
    )
    return (layer_out, input_grad, *totals, norms[0][None], norms[1][None])


def solution(mesh):
    return jax.shard_map(
        on_device,
        mesh=mesh,
        in_specs=(
            P("section", None, ("dp", "tensor"), None),
            P(None, None, "dp", None),
            P(None, ("dp", "tensor"), None),
            P("section", None, "tensor"),
            P("section", "tensor", None),
            P("section", None, "tensor"),
            P("section", None, "tensor"),
            P("section", "tensor", None),
            P("section", None, None),
            P("section", None, None),
        ),
        out_specs=(
            P("section", None, ("dp", "tensor"), None),
            P("section", None, ("dp", "tensor"), None),
            P("section", None, "tensor"),
            P("section", "tensor", None),
            P("section", None, "tensor"),
            P("section", None, "tensor"),
            P("section", "tensor", None),
            P("section", None, "tensor"),
            P("section", None, "tensor"),
        ),
        check_vma=False,
    )
```

```python
import math

import jax
import jax.numpy as jnp
from jax import lax
from jax.experimental import pallas as pl
from jax.experimental.pallas import tpu as pltpu
from jax.sharding import PartitionSpec as P

HD = 64
EPS = 1e-05
MASKED = -1e30
BF = jnp.bfloat16
F32 = jnp.float32
VMEM_SPARE = 6 * 1024 * 1024
GELU_C = 0.7071067811865476
PHI_C = 0.3989422804014327


LIGHT = pl.CostEstimate(flops=1024, bytes_accessed=1024, transcendentals=0)


def mm(a, b):
    return jnp.dot(a, b, preferred_element_type=F32)


def mm_bt(a, b):
    return lax.dot_general(a, b, (((1,), (1,)), ((), ())), preferred_element_type=F32)


def mm_at(a, b):
    return lax.dot_general(a, b, (((0,), (0,)), ((), ())), preferred_element_type=F32)


def spec(shape, dtype=BF):
    return jax.ShapeDtypeStruct(shape, dtype)


class Saved:
    def __init__(self, shape, dtype=BF):
        self.shape, self.dtype, self.size = shape, jnp.dtype(dtype), math.prod(shape)


def in_hbm(array):
    return pltpu.with_memory_space_constraint(array, pltpu.HBM)


class Near:
    def __init__(self, shape, p, q=None, at=0):
        self.shape, self.p, self.q, self.at = shape, p, q, at
        self.dtype, self.size = p.dtype, shape[0] * shape[1]


STRICT = [True]
ORDER = []


def in_order(deps):
    return (*deps, *ORDER[-1:]) if STRICT[-1] else tuple(deps)


def note(results):
    ORDER.append(results[0] if isinstance(results, (tuple, list)) else results)
    return results


def sectioned(
    body, core, flags, small, big, outs, scratch, flops, trans=0, deps=(), owners=None, sums=()
):
    deps = in_order(deps)
    terms = [array for chain in sums for array in (chain.value, chain.got)]
    n_terms = len(terms)
    sources, places = [], []
    for i, array in enumerate(big):
        if isinstance(array, Near) and array.q is None:
            places.append((i, array.shape[0], array.at, None))
            sources.append(array.p)
        elif isinstance(array, Near):
            half = array.shape[0] // 2
            for turn, part in enumerate((array.p, array.q)):
                places.append((i, half, array.at, turn))
                sources.append(part)
        else:
            places.append((i, None, None, None))
            sources.append(array)
    n_small, n_big, n_deps, n_out = len(small), len(big), len(deps), len(outs)
    n_src = len(sources)

    def kernel(flags_ref, *refs):
        small_refs = refs[:n_small]
        big_hbm = refs[n_small : n_small + n_src]
        at = n_small + n_src
        term_hbm = refs[at : at + n_terms]
        at += n_terms + n_deps
        out_hbm = refs[at : at + n_out]
        at += n_out
        sum_hbm = refs[at : at + len(sums)]
        at += len(sums)
        big_refs = refs[at : at + n_big]
        at += n_big
        out_refs = refs[at : at + n_out]
        at += n_out
        term_refs = refs[at : at + n_terms]
        at += n_terms
        extra = refs[at:-4]
        in_sem, out_sem, term_sem, sum_sem = refs[-4:]

        def start_sums():
            loads = [
                pltpu.make_async_copy(term_hbm[i], term_refs[i], term_sem.at[i])
                for i in range(n_terms)
            ]
            for load in loads:
                load.start()
            return loads

        def end_sums(loads):
            stores = []
            for i in range(len(sums)):
                loads[2 * i].wait()
                loads[2 * i + 1].wait()
                a_ref, b_ref = term_refs[2 * i], term_refs[2 * i + 1]
                chunk = 64 if a_ref.shape[0] % 64 == 0 else a_ref.shape[0]

                @pl.loop(0, a_ref.shape[0] // chunk)
                def _(r):
                    at = pl.ds(pl.multiple_of(r * chunk, chunk), chunk)
                    a_ref[at, :] = (a_ref[at, :].astype(F32) + b_ref[at, :].astype(F32)).astype(BF)

                stores.append(pltpu.make_async_copy(a_ref, sum_hbm[i], sum_sem.at[i]))
                stores[-1].start()
            return stores

        def run():
            copies = [[] for _ in range(n_big)]
            for s, (i, half, first, turn) in enumerate(places):
                if half is None:
                    copy = pltpu.make_async_copy(big_hbm[s], big_refs[i], in_sem.at[s])
                elif turn is None:
                    copy = pltpu.make_async_copy(
                        big_hbm[s].at[pl.ds(first, half), :], big_refs[i], in_sem.at[s]
                    )
                else:
                    odd = flags_ref[1] if turn == 0 else 1 - flags_ref[1]
                    copy = pltpu.make_async_copy(
                        big_hbm[s].at[pl.ds(first, half), :],
                        big_refs[i].at[pl.ds(pl.multiple_of(odd * half, half), half), :],
                        in_sem.at[s],
                    )
                if owners is None:
                    copy.start()
                else:
                    pl.when(flags_ref[0] == owners[i])(copy.start)
                copies[i].append(copy)
            done = [
                pltpu.make_async_copy(out_refs[i], out_hbm[i], out_sem.at[i]) for i in range(n_out)
            ]
            loads = start_sums() if sums and core is not None else None
            body(
                flags_ref, small_refs, big_refs, out_refs, extra,
                lambda *which: [copy.wait() for i in which for copy in copies[i]],
                lambda *which: [done[i].start() for i in which],
            )
            if loads:
                done.extend(end_sums(loads))
            for copy in done:
                copy.wait()

        if core is None:
            run()
        else:
            pl.when(flags_ref[0] == core)(run)
        if sums and core is None:

            @pl.when(flags_ref[0] == sums[0].core)
            def _():
                for copy in end_sums(start_sums()):
                    copy.wait()

    nbytes = sum(a.size * a.dtype.itemsize for a in (*big, *outs))
    nbytes += sum(a.size * 2 for a in terms)
    held = nbytes + sum(math.prod(a.shape) * jnp.dtype(a.dtype).itemsize for a in scratch)
    results = note(pl.pallas_call(
        kernel,
        out_shape=tuple(pltpu.HBM(a.shape, a.dtype) if isinstance(a, Saved) else a for a in outs)
        + tuple(spec(chain.value.shape) for chain in sums),
        in_specs=[pl.BlockSpec(memory_space=pltpu.SMEM)]
        + [pl.BlockSpec(memory_space=pltpu.VMEM)] * n_small
        + [pl.BlockSpec(memory_space=pl.ANY)] * (n_src + n_terms + n_deps),
        out_specs=tuple(
            pl.BlockSpec(memory_space=pltpu.HBM if isinstance(a, Saved) else pl.ANY) for a in outs
        )
        + tuple([pl.BlockSpec(memory_space=pl.ANY)] * len(sums)),
        scratch_shapes=[pltpu.VMEM(a.shape, a.dtype) for a in (*big, *outs)]
        + [pltpu.VMEM(a.shape, BF) for a in terms]
        + list(scratch)
        + [
            pltpu.SemaphoreType.DMA((max(1, n_src),)), pltpu.SemaphoreType.DMA((n_out,)),
            pltpu.SemaphoreType.DMA((max(1, n_terms),)),
            pltpu.SemaphoreType.DMA((max(1, len(sums)),)),
        ],
        compiler_params=pltpu.CompilerParams(vmem_limit_bytes=int(held) + VMEM_SPARE),
        cost_estimate=LIGHT,
    )(flags, *small, *sources, *terms, *deps))
    for chain, value in zip(sums, results[n_out:]):
        chain.forward(value)
    return results[:n_out]


def norm_rows(terms, gain, bias, x_ref, hat_ref, inv_ref, chunk=32):
    rows, width = x_ref.shape

    @pl.loop(0, rows // chunk, unroll=4)
    def _(i):
        at = pl.ds(pl.multiple_of(i * chunk, chunk), chunk)
        v = sum(term[at, :].astype(F32) for term in terms)
        centre = v - jnp.mean(v, axis=-1, keepdims=True)
        inv = lax.rsqrt(jnp.mean(centre * centre, axis=-1, keepdims=True) + EPS)
        hat = centre * inv
        x_ref[at, :] = (hat * gain[...] + bias[...]).astype(BF)
        if hat_ref is not None:
            hat_ref[at, :] = hat.astype(BF)
            inv_ref[at, :] = jnp.broadcast_to(inv, (chunk, 128))


def norm_back_rows(terms, hat_ref, inv_ref, gain, dv_ref, n_ref, chunk=32):
    rows, width = dv_ref.shape

    def step(i, sums):
        at = pl.ds(pl.multiple_of(i * chunk, chunk), chunk)
        dy = sum(term[at, :].astype(F32) for term in terms)
        hat = hat_ref[at, :].astype(F32)
        t = dy * gain[...]
        dv = (
            t
            - jnp.mean(t, axis=-1, keepdims=True)
            - hat * jnp.mean(t * hat, axis=-1, keepdims=True)
        ) * inv_ref[at, :1]
        dv_ref[at, :] = dv.astype(BF)
        return (
            sums[0] + (dy * hat).reshape(chunk // 8, 8, width).sum(0),
            sums[1] + dy.reshape(chunk // 8, 8, width).sum(0),
        )

    zero = jnp.zeros((8, width), F32)
    n_ref[0], n_ref[1] = lax.fori_loop(0, rows // chunk, step, (zero, zero), unroll=4)


def matmul_into(x_ref, w_ref, out_ref, at=0, tile=256):
    columns = w_ref.shape[1]
    tile = min(tile, columns)
    for c in range(0, columns, tile):
        out_ref[:, at + c : at + c + tile] = mm(x_ref[...], w_ref[:, c : c + tile]).astype(BF)


def matmul_bt_into(x_ref, w_ref, out_ref, at=0, tile=256):
    rows = w_ref.shape[0]
    tile = min(tile, rows)
    for c in range(0, rows, tile):
        out_ref[:, at + c : at + c + tile] = mm_bt(x_ref[...], w_ref[c : c + tile, :]).astype(BF)


def attend(heads, length, step, offsets, o_step, causal, q_ref, kv_ref, segq, segk, o_ref, lse_ref, bias_ref):
    q_off, k_off, v_off, o_off = offsets
    tile = min(256, length)
    if o_step != HD:
        o_ref[...] = jnp.zeros_like(o_ref)
    lse_ref[...] = jnp.zeros_like(lse_ref)
    for p in range(q_ref.shape[0] // length):
        base = p * length
        all_rows = slice(base, base + length)
        same = segq[all_rows, :] == segk[p : p + 1, :]
        if causal is not None:
            rows = lax.broadcasted_iota(jnp.int32, (length, length), 0)
            cols = lax.broadcasted_iota(jnp.int32, (length, length), 1)
            same = same & (cols * causal <= rows)
        bias_ref[...] = jnp.where(same, 0.0, MASKED)
        for h in range(heads):
            k = kv_ref[all_rows, h * step + k_off : h * step + k_off + HD]
            v = kv_ref[all_rows, h * step + v_off : h * step + v_off + HD]
            for r in range(0, length, tile):
                at = slice(base + r, base + r + tile)
                q = q_ref[at, h * step + q_off : h * step + q_off + HD] * jnp.asarray(HD**-0.5, BF)
                s = mm_bt(q, k) + bias_ref[r : r + tile, :]
                top = jnp.max(s, axis=-1, keepdims=True)
                e = jnp.exp(s - top)
                total = jnp.sum(e, axis=-1, keepdims=True)
                prob = (e * (1.0 / total)).astype(BF)
                o_ref[at, h * o_step + o_off : h * o_step + o_off + HD] = mm(prob, v).astype(BF)
                lse_ref[at, h : h + 1] = top + jnp.log(total)


def attend_back(
    heads, length, step, offsets, o_step, causal, q_ref, kv_ref, segq, segk, o_ref, lse_ref, do_ref,
    dq_ref, dkv_ref, bias_ref, inner_ref,
):
    q_off, k_off, v_off, o_off = offsets
    tile = min(256, length)
    if dq_ref is not dkv_ref:
        dq_ref[...] = jnp.zeros_like(dq_ref)
    for p in range(q_ref.shape[0] // length):
        base = p * length
        all_rows = slice(base, base + length)
        same = segk[all_rows, :] == segq[p : p + 1, :]
        if causal is not None:
            keys = lax.broadcasted_iota(jnp.int32, (length, length), 0)
            queries = lax.broadcasted_iota(jnp.int32, (length, length), 1)
            same = same & (keys * causal <= queries)
        bias_ref[...] = jnp.where(same, 0.0, MASKED)
        inner_ref[...] = jnp.zeros_like(inner_ref)
        for h in range(heads):
            cols = slice(h * o_step + o_off, h * o_step + o_off + HD)
            prod = do_ref[all_rows, cols].astype(F32) * o_ref[all_rows, cols].astype(F32)
            inner_ref[:, h : h + 1] = jnp.sum(prod, axis=-1, keepdims=True)
        inner_t = jnp.transpose(inner_ref[...])
        lse_t = jnp.transpose(lse_ref[all_rows, :])
        for h in range(heads):
            q_cols = slice(h * step + q_off, h * step + q_off + HD)
            k_cols = slice(h * step + k_off, h * step + k_off + HD)
            v_cols = slice(h * step + v_off, h * step + v_off + HD)
            q = q_ref[all_rows, q_cols] * jnp.asarray(HD**-0.5, BF)
            do = do_ref[all_rows, h * o_step + o_off : h * o_step + o_off + HD]
            dq = jnp.zeros((length, HD), F32)
            for r in range(0, length, tile):
                rows = slice(base + r, base + r + tile)
                k = kv_ref[rows, k_cols]
                v = kv_ref[rows, v_cols]
                s = mm_bt(k, q) + bias_ref[r : r + tile, :]
                prob = jnp.exp(s - lse_t[h : h + 1, :])
                dkv_ref[rows, v_cols] = mm(prob.astype(BF), do).astype(BF)
                ds = (prob * (mm_bt(v, do) - inner_t[h : h + 1, :])).astype(BF)
                dkv_ref[rows, k_cols] = mm(ds, q).astype(BF)
                dq = dq + mm_at(ds, k)
            dq_ref[all_rows, q_cols] = (dq * HD**-0.5).astype(BF)


SELF_AT = (0, HD, 2 * HD, 0)
CROSS_AT = (0, 0, HD, HD)


def self_forward(flags, src, seg, gain, bias, w_qkv, w_out, deps=()):
    packed, length = seg.shape
    rows, width = src.shape
    heads = 2 * w_out[0].shape[0] // HD
    part = w_qkv[0].shape[1]

    def body(flags, small, big, outs, extra, wait, flush):
        segq, segk, gain, bias = small
        src, qkv_a, qkv_b, out_a, out_b = big
        x, hat, inv, qkv, o, lse, partial = outs
        (mask,) = extra
        wait(0)

        @pl.when(flags[0] == 0)
        def _():
            norm_rows([src], gain, bias, x, hat, inv)

        @pl.when(flags[0] != 0)
        def _():
            x[...] = src[...]

        flush(0, 1, 2)
        wait(1)
        matmul_into(x, qkv_a, qkv)
        wait(2)
        matmul_into(x, qkv_b, qkv, part)
        flush(3)
        attend(heads, length, 3 * HD, SELF_AT, HD, flags[0], qkv, qkv, segq, segk, o, lse, mask)
        flush(4, 5)
        wait(3, 4)
        half = heads // 2 * HD
        for c in range(0, width, 256):
            partial[:, c : c + 256] = (
                mm(o[:, :half], out_a[:, c : c + 256]) + mm(o[:, half:], out_b[:, c : c + 256])
            ).astype(BF)
        flush(6)

    return sectioned(
        body, None, flags,
        (seg.reshape(rows, 1), seg, gain, bias),
        (src, *w_qkv, *w_out),
        (
            spec((rows, width)), Saved((rows, width)), Saved((rows, 128), F32),
            Saved((rows, 2 * part)), Saved((rows, heads * HD)), Saved((rows, 128), F32),
            spec((rows, width)),
        ),
        [pltpu.VMEM((length, length), F32)],
        2 * rows * width * heads * HD * 4 + 16 * heads * rows * length * HD,
        heads * rows * length, deps,
    )


def ffn_forward(core, flags, res, pair, gain, bias, w_up, w_down, deps=()):
    rows, width = res.shape
    part = w_up[0].shape[1]
    tile = min(512, part)

    def body(flags, small, big, outs, extra, wait, flush):
        gain, bias = small
        res, own, got, up_a, up_b, down_a, down_b = big
        x, hat, inv, hidden, slope, partial = outs
        (total,) = extra
        wait(0, 1, 2)
        norm_rows([res, own, got], gain, bias, x, hat, inv)
        flush(0, 1, 2)
        for i, (up, down) in enumerate(((up_a, down_a), (up_b, down_b))):
            wait(3 + i, 5 + i)
            for c in range(0, part, tile):
                at = slice(i * part + c, i * part + c + tile)
                u = mm(x[...], up[:, c : c + tile])
                phi = 0.5 * (1.0 + lax.erf(u * GELU_C))
                slope[:, at] = (phi + u * (PHI_C * jnp.exp(-0.5 * u * u))).astype(BF)
                hidden[:, at] = (u * phi).astype(BF)
                term = mm(hidden[:, at], down[c : c + tile, :])
                if i == 0 and c == 0:
                    total[...] = term
                else:
                    total[...] += term
        partial[...] = total[...].astype(BF)
        flush(3, 4, 5)

    return sectioned(
        body, core, flags, (gain, bias), (res, *pair, *w_up, *w_down),
        (
            spec((rows, width)), Saved((rows, width)), Saved((rows, 128), F32),
            Saved((rows, 2 * part)), Saved((rows, 2 * part)), spec((rows, width)),
        ),
        [pltpu.VMEM((rows, width), F32)],
        8 * rows * width * part, rows * part * 4, deps,
    )


def norm_project(core, flags, res, pair, gain, bias, w, deps=()):
    rows, width = res.shape
    part = w[0].shape[1]

    def body(flags, small, big, outs, extra, wait, flush):
        gain, bias = small
        res, own, got, w_a, w_b = big
        x, hat, inv, proj = outs
        wait(0, 1, 2)
        norm_rows([res, own, got], gain, bias, x, hat, inv)
        flush(0, 1, 2)
        wait(3)
        matmul_into(x, w_a, proj)
        wait(4)
        matmul_into(x, w_b, proj, part)
        flush(3)

    return sectioned(
        body, core, flags, (gain, bias), (res, *pair, *w),
        (spec((rows, width)), Saved((rows, width)), Saved((rows, 128), F32), spec((rows, 2 * part))),
        [], 4 * rows * width * part, 0, deps,
    )


def cross_forward(core, flags, q, kv, segq, segk, w, deps=()):
    packed, length = segq.shape
    rows = q.shape[0]
    width, part = w[0].shape
    heads = 2 * part // (2 * HD)

    def body(flags, small, big, outs, extra, wait, flush):
        segq, segk = small
        q, kv, w_a, w_b = big
        c, lse, partial = outs
        (mask,) = extra
        wait(0, 1)
        attend(heads, length, 2 * HD, CROSS_AT, 2 * HD, None, q, kv, segq, segk, c, lse, mask)
        flush(0, 1)
        wait(2, 3)
        for r in range(0, width, 256):
            partial[:, r : r + 256] = (
                mm_bt(c[:, :part], w_a[r : r + 256, :]) + mm_bt(c[:, part:], w_b[r : r + 256, :])
            ).astype(BF)
        flush(2)

    return sectioned(
        body, core, flags, (segq.reshape(rows, 1), segk), (q, kv, *w),
        (Saved((rows, 2 * part)), Saved((rows, 128), F32), spec((rows, width))),
        [pltpu.VMEM((length, length), F32)],
        4 * rows * width * part + 16 * heads * rows * length * HD, heads * rows * length, deps,
    )


def ffn_back_loop(df, slope, up, down, du, total, partial, wait, first):
    part = up[0].shape[1]
    tile = min(512, part)
    for i in range(2):
        wait(first + i, first + 2 + i)
        for c in range(0, part, tile):
            at = slice(i * part + c, i * part + c + tile)
            dh = mm_bt(df[...], down[i][c : c + tile, :])
            du[:, at] = (dh * slope[:, at].astype(F32)).astype(BF)
            term = mm_bt(du[:, at], up[i][:, c : c + tile])
            if i == 0 and c == 0:
                total[...] = term
            else:
                total[...] += term
    partial[...] = total[...].astype(BF)


def top_backward(core, flags, res, pair, cot, gain, bias, slope, w_up, w_down, deps=()):
    rows, width = res.shape
    part = w_up[0].shape[1]

    def body(flags, small, big, outs, extra, wait, flush):
        gain, bias = small
        res, own, got, cot, slope, up_a, up_b, down_a, down_b = big
        y, df, n, du, partial = outs
        total, hat, inv = extra
        wait(0, 1, 2)
        norm_rows([res, own, got], gain, bias, y, hat, inv)
        flush(0)
        wait(3)
        norm_back_rows([cot], hat, inv, gain, df, n)
        flush(1, 2)
        wait(4)
        ffn_back_loop(df, slope, (up_a, up_b), (down_a, down_b), du, total, partial, wait, 5)
        flush(3, 4)

    return sectioned(
        body, core, flags, (gain, bias), (res, *pair, in_hbm(cot), in_hbm(slope), *w_up, *w_down),
        (
            Saved((rows, width)), spec((rows, width)), Saved((2, 8, width), F32),
            Saved((rows, 2 * part)), spec((rows, width)),
        ),
        [pltpu.VMEM((rows, width), F32), pltpu.VMEM((rows, width), BF), pltpu.VMEM((rows, 128), F32)],
        8 * rows * width * part, 0, deps,
    )


def ffn_backward(core, flags, terms, kept, gain, slope, w_up, w_down, deps=()):
    rows, width = terms[0].shape
    part = w_up[0].shape[1]
    k = len(terms)

    def body(flags, small, big, outs, extra, wait, flush):
        (gain,) = small
        terms = big[:k]
        hat, inv, slope, up_a, up_b, down_a, down_b = big[k:]
        df, n, du, partial = outs
        (total,) = extra
        wait(*range(k + 2))
        norm_back_rows(terms, hat, inv, gain, df, n)
        flush(0, 1)
        wait(k + 2)
        ffn_back_loop(df, slope, (up_a, up_b), (down_a, down_b), du, total, partial, wait, k + 3)
        flush(2, 3)

    return sectioned(
        body, core, flags, (gain,), (*terms, *map(in_hbm, kept), in_hbm(slope), *w_up, *w_down),
        (
            spec((rows, width)), Saved((2, 8, width), F32), Saved((rows, 2 * part)),
            spec((rows, width)),
        ),
        [pltpu.VMEM((rows, width), F32)],
        8 * rows * width * part, 0, deps,
    )


def cross_backward(core, flags, terms, kept, gain, q, kv, segq, segk, c, lse, w, deps=()):
    packed, length = segq.shape
    rows, width = terms[0].shape
    part = w[0].shape[1]
    heads = 2 * part // (2 * HD)
    k = len(terms)

    def body(flags, small, big, outs, extra, wait, flush):
        segq, segk, gain = small
        terms = big[:k]
        hat, inv, w_a, w_b, q, kv, c, lse = big[k:]
        dca, n, dq, dkv, partial = outs
        dc, mask, inner = extra
        wait(*range(k + 2))
        norm_back_rows(terms, hat, inv, gain, dca, n)
        flush(0, 1)
        wait(k + 2, k + 3)
        matmul_into(dca, w_a, dc)
        matmul_into(dca, w_b, dc, part)
        wait(*range(k + 4, k + 8))
        attend_back(
            heads, length, 2 * HD, CROSS_AT, 2 * HD, None, q, kv, segq, segk, c, lse, dc, dq, dkv,
            mask, inner,
        )
        flush(2, 3)
        for r in range(0, width, 256):
            partial[:, r : r + 256] = (
                mm_bt(dq[:, :part], w_a[r : r + 256, :]) + mm_bt(dq[:, part:], w_b[r : r + 256, :])
            ).astype(BF)
        flush(4)

    return sectioned(
        body, core, flags, (segq, segk.reshape(rows, 1), gain),
        (*terms, *map(in_hbm, kept), *w, *map(in_hbm, (q, kv, c, lse))),
        (
            spec((rows, width)), Saved((2, 8, width), F32), Saved((rows, 2 * part)),
            spec((rows, 2 * part)), spec((rows, width)),
        ),
        [
            pltpu.VMEM((rows, 2 * part), BF), pltpu.VMEM((length, length), F32),
            pltpu.VMEM((length, 128), F32),
        ],
        8 * rows * width * part + 40 * heads * rows * length * HD, heads * rows * length, deps,
    )


def memory_backward(core, flags, dkv, w, deps=()):
    rows = dkv.shape[0]
    width, part = w[0].shape

    def body(flags, small, big, outs, extra, wait, flush):
        dkv, w_a, w_b = big
        (partial,) = outs
        wait(0, 1, 2)
        for r in range(0, width, 256):
            partial[:, r : r + 256] = (
                mm_bt(dkv[:, :part], w_a[r : r + 256, :]) + mm_bt(dkv[:, part:], w_b[r : r + 256, :])
            ).astype(BF)
        flush(0)

    return sectioned(
        body, core, flags, (), (dkv, *w), (spec((rows, width)),), [], 4 * rows * width * part, 0, deps
    )[0]


def self_backward(
    core, flags, terms, kept, gain, qkv, o, lse, seg, w_qkv, w_out, deps=(), sums=()
):
    packed, length = seg.shape
    rows, width = terms[0].shape
    heads = 2 * w_out[0].shape[0] // HD
    part = w_qkv[0].shape[1]
    k = len(terms)

    def body(flags, small, big, outs, extra, wait, flush):
        segq, segk, gain = small
        terms = big[:k]
        hat, inv, out_a, out_b, qkv, o, lse, qkv_a, qkv_b = big[k:]
        ds, n, dqkv, partial = outs
        do, mask, inner = extra
        wait(*range(k + 2))
        norm_back_rows(terms, hat, inv, gain, ds, n)
        flush(0, 1)
        wait(k + 2, k + 3)
        half = heads // 2 * HD
        matmul_bt_into(ds, out_a, do)
        matmul_bt_into(ds, out_b, do, half)
        wait(*range(k + 4, k + 7))
        attend_back(
            heads, length, 3 * HD, SELF_AT, HD, flags[0], qkv, qkv, segq, segk, o, lse, do, dqkv,
            dqkv, mask, inner,
        )
        flush(2)
        wait(k + 7, k + 8)
        for r in range(0, width, 256):
            partial[:, r : r + 256] = (
                mm_bt(dqkv[:, :part], qkv_a[r : r + 256, :])
                + mm_bt(dqkv[:, part:], qkv_b[r : r + 256, :])
            ).astype(BF)
        flush(3)

    return sectioned(
        body, core, flags, (seg, seg.reshape(rows, 1), gain),
        (*terms, *map(in_hbm, kept), *w_out, *map(in_hbm, (qkv, o, lse)), *w_qkv),
        (
            spec((rows, width)), Saved((2, 8, width), F32), Saved((rows, 2 * part)),
            spec((rows, width)),
        ),
        [
            pltpu.VMEM((rows, heads * HD), BF), pltpu.VMEM((length, length), F32),
            pltpu.VMEM((length, 128), F32),
        ],
        2 * rows * width * heads * HD * 4 + 40 * heads * rows * length * HD,
        heads * rows * length, deps, sums=sums,
    )


def weight_grads(flags, groups, deps=(), cuts=1, sums=()):
    lists = [
        in_hbm(array) for own in groups for lefts, rights, _ in own for array in (*lefts, *rights)
    ]
    live = [core for core in range(2) if groups[core]]
    some = groups[live[0]]
    height = some[0][0][0].shape[1] // (2 if some[0][2] else 1)
    widths = [
        [rights[0].shape[1] // (1 if split_left else 2) for _, rights, split_left in own]
        for own in groups
    ]
    piece = height // cuts
    counts = [sum(2 * len(lefts) for lefts, _, _ in own) for own in groups]

    def body(flags, small, big, outs, extra, wait, flush):
        def run(core):
            for i in reversed(range(2)):
                first, at = counts[0] * core, 0
                for g, (lefts, rights, split_left) in enumerate(groups[core]):
                    k = len(lefts)
                    if i == 1:
                        wait(*range(first, first + 2 * k))
                    i_m = i * height if split_left else 0
                    n = widths[core][g]
                    i_n = 0 if split_left else i * n
                    tile = min(256, piece)
                    for r in range(0, height, tile):
                        low = r % piece
                        outs[i * cuts + r // piece][low : low + tile, at : at + n] = sum(
                            mm_at(
                                big[first + j][:, i_m + r : i_m + r + tile],
                                big[first + k + j][:, i_n : i_n + n],
                            )
                            for j in range(k)
                        ).astype(BF)
                    first += 2 * k
                    at += n
                flush(*range(i * cuts, (i + 1) * cuts))

        if len(live) == 1:
            run(live[0])
        else:
            for core in live:
                pl.when(flags[0] == core)(lambda core=core: run(core))

    blocks = tuple(spec((piece, sum(widths[live[0]]))) for _ in range(2 * cuts))
    owners = [0] * counts[0] + [1] * counts[1]
    return sectioned(
        body, live[0] if len(live) == 1 else None, flags, (), lists, blocks, [], 0, 0, deps, owners,
        sums,
    )


def after(array, *deps):
    deps = in_order(deps)
    return note(pl.pallas_call(
        lambda *refs: None,
        out_shape=spec(array.shape, array.dtype),
        in_specs=[pl.BlockSpec(memory_space=pl.ANY)] * (1 + len(deps)),
        out_specs=pl.BlockSpec(memory_space=pl.ANY),
        input_output_aliases={0: 0},
        cost_estimate=LIGHT,
    )(array, *deps))


def pack_rows(flags, weights, deps=(), whole=False):
    deps = in_order(deps)
    halves = [w.shape[0] // (1 if whole else 2) for w in weights]
    out = spec((sum(halves), weights[0].shape[1]))

    def kernel(flags_ref, *refs):
        target, sem = refs[-2:]
        copies, at = [], 0
        for i, half in enumerate(halves):
            first = 0 if whole else pl.multiple_of(flags_ref[1] * half, half)
            copies.append(
                pltpu.make_async_copy(
                    refs[i].at[pl.ds(first, half), :], target.at[pl.ds(at, half), :], sem.at[i]
                )
            )
            at += half
        for copy in copies:
            copy.start()
        for copy in copies:
            copy.wait()

    return note(pl.pallas_call(
        kernel,
        out_shape=out,
        in_specs=[pl.BlockSpec(memory_space=pltpu.SMEM)]
        + [pl.BlockSpec(memory_space=pl.ANY)] * (len(weights) + len(deps)),
        out_specs=pl.BlockSpec(memory_space=pltpu.VMEM),
        scratch_shapes=[pltpu.SemaphoreType.DMA((len(weights),))],
        cost_estimate=LIGHT,
    )(flags, *weights, *deps))


def add_pairs(flags, pairs, deps=()):
    deps = in_order(deps)
    k = len(pairs)
    cuts = [4 if a.shape[0] % 64 == 0 else 1 for _, a, _ in pairs]

    def kernel(flags_ref, *refs):
        terms = refs[: 2 * k]
        outs = refs[2 * k + len(deps) : 3 * k + len(deps)]
        held = refs[3 * k + len(deps) : -2]
        in_sem, out_sem = refs[-2:]
        jobs = []
        for p, (core, a, _) in enumerate(pairs):
            live = flags_ref[0] >= 0 if core is None else flags_ref[0] == core
            chunk = a.shape[0] // cuts[p]
            for i in range(cuts[p]):
                at = pl.ds(i * chunk, chunk)
                loads = [
                    pltpu.make_async_copy(
                        terms[2 * p + j].at[at, :], held[2 * p + j].at[at, :], in_sem.at[2 * p + j, i]
                    )
                    for j in range(2)
                ]
                store = pltpu.make_async_copy(held[2 * p].at[at, :], outs[p].at[at, :], out_sem.at[p, i])
                jobs.append((live, at, held[2 * p], held[2 * p + 1], loads, store))
        for live, _, _, _, loads, _ in jobs:

            @pl.when(live)
            def _():
                for load in loads:
                    load.start()

        for live, at, a_ref, b_ref, loads, store in jobs:

            @pl.when(live)
            def _():
                for load in loads:
                    load.wait()
                a_ref[at, :] = (a_ref[at, :].astype(F32) + b_ref[at, :].astype(F32)).astype(BF)
                store.start()

        for live, _, _, _, _, store in jobs:
            pl.when(live)(store.wait)

    arrays = [array for _, a, b in pairs for array in (a, b)]
    return note(pl.pallas_call(
        kernel,
        out_shape=tuple(spec(a.shape) for _, a, _ in pairs),
        in_specs=[pl.BlockSpec(memory_space=pltpu.SMEM)]
        + [pl.BlockSpec(memory_space=pl.ANY)] * (2 * k + len(deps)),
        out_specs=tuple([pl.BlockSpec(memory_space=pl.ANY)] * k),
        scratch_shapes=[pltpu.VMEM(array.shape, BF) for array in arrays]
        + [pltpu.SemaphoreType.DMA((2 * k, 4)), pltpu.SemaphoreType.DMA((k, 4))],
        compiler_params=pltpu.CompilerParams(
            vmem_limit_bytes=sum(2 * array.size for array in arrays) + VMEM_SPARE
        ),
        cost_estimate=LIGHT,
    )(flags, *arrays, *deps))


def finish(flags, kept, got, columns, deps=()):
    deps = in_order(deps)
    sources = [kept[0], kept[1], got[0], got[1]]
    rows = sum(piece.shape[0] for piece in sources[0][0])
    cuts = 4 if rows % 64 == 0 else max(len(pieces) for pieces, _ in sources)
    chunk = rows // cuts
    flat = [in_hbm(piece) for pieces, _ in sources for piece in pieces]

    def kernel(flags_ref, *refs):
        out_hbm, low_ref, out_ref, in_sem, out_sem = refs[len(flat) + len(deps) :]
        loads, stores = [], []
        for i in range(cuts):
            at = pl.ds(i * chunk, chunk)
            first_ref = 0
            for c, (pieces, first) in enumerate(sources):
                size = rows // len(pieces)
                load = pltpu.make_async_copy(
                    refs[first_ref + i * chunk // size].at[
                        pl.ds(i * chunk % size, chunk), pl.ds(first, columns)
                    ],
                    low_ref.at[at, :],
                    in_sem.at[i],
                )
                pl.when(flags_ref[0] + 2 * flags_ref[2] == c)(load.start)
                first_ref += len(pieces)
            loads.append(load)
            stores.append(pltpu.make_async_copy(out_ref.at[at, :], out_hbm.at[at, :], out_sem.at[i]))
        for i in range(cuts):
            at = pl.ds(i * chunk, chunk)
            loads[i].wait()
            out_ref[at, :] = low_ref[at, :].astype(F32)
            stores[i].start()
        for store in stores:
            store.wait()

    out = spec((rows, columns), F32)
    return note(pl.pallas_call(
        kernel,
        out_shape=out,
        in_specs=[pl.BlockSpec(memory_space=pltpu.SMEM)]
        + [pl.BlockSpec(memory_space=pl.ANY)] * (len(flat) + len(deps)),
        out_specs=pl.BlockSpec(memory_space=pl.ANY),
        scratch_shapes=[
            pltpu.VMEM(out.shape, BF), pltpu.VMEM(out.shape, F32),
            pltpu.SemaphoreType.DMA((cuts,)), pltpu.SemaphoreType.DMA((cuts,)),
        ],
        compiler_params=pltpu.CompilerParams(vmem_limit_bytes=6 * rows * columns + VMEM_SPARE),
        cost_estimate=LIGHT,
    )(flags, *flat, *deps))


def norm_back(dy, kept, gain):
    hat, inv = kept
    t = dy * gain
    dv = (
        t
        - jnp.mean(t, axis=-1, keepdims=True)
        - hat * jnp.mean(t * hat, axis=-1, keepdims=True)
    ) * inv
    return dv, jnp.stack([jnp.sum(dy * hat, axis=0), jnp.sum(dy, axis=0)])


def on_device(
    layer_in, segments, cotangent, self_qkv, self_out, cross_proj, ffn_up, ffn_down,
    norm_gain, norm_bias,
):
    ORDER.clear()
    STRICT[-1] = True
    sec = lax.axis_index("section")
    n = lax.axis_size("tensor")
    zs = lax.axis_size("dp")
    z = lax.axis_index("dp")
    t = lax.axis_index("tensor")
    tp = n // 2
    bits = tp.bit_length() - 1
    x = t % tp
    fs = t // tp
    micro, share, width = layer_in.shape[1:]
    packed, length = segments.shape[2:]
    rows = packed * length
    assert micro == 4 and zs == 4
    is0 = sec == 0
    gain, bias = norm_gain[0], norm_bias[0]

    def to_core(v, core):
        return lax.ppermute(v, "section", [(1 - core, core)])

    def flip(v, bit, core=None):
        if core is None:
            return lax.ppermute(v, "tensor", [(i, i ^ (1 << bit)) for i in range(n)])
        return lax.ppermute(
            v,
            ("section", "tensor"),
            [(core * n + i, core * n + (i ^ (1 << bit))) for i in range(n)],
        )

    def z_on(v, core, pairs):
        if core is None:
            return lax.ppermute(v, "dp", pairs)
        if core is None:
            return lax.ppermute(v, "dp", pairs)
        if core is None:
            return lax.ppermute(v, "dp", pairs)
        return lax.ppermute(v, ("section", "dp"), [(core * zs + a, core * zs + b) for a, b in pairs])

    def tp_sum(v, core=None):
        for bit in range(bits):
            got = flip(v, bit, core)
            if bit < bits - 1:
                v = (v.astype(F32) + got.astype(F32)).astype(BF)
        return v, got

    def tp_scatter(v, core):
        cur = v.reshape(2, tp, share, width)
        for bit in reversed(range(bits)):
            half = 1 << bit
            bit_on = (x >> bit) & 1
            parts = cur.reshape(2, 2, half, share, width)
            give = lax.dynamic_index_in_dim(parts, 1 - bit_on, 1, keepdims=False)
            keep = lax.dynamic_index_in_dim(parts, bit_on, 1, keepdims=False)
            total = keep.astype(F32) + flip(give, bit, core).astype(F32)
            cur = total.astype(BF)
        return total.reshape(2 * share, width)

    def own_rows(v):
        return lax.dynamic_index_in_dim(
            v.reshape(2, tp, share, v.shape[-1]), x, 1, keepdims=False
        ).reshape(2 * share, v.shape[-1])

    def ordered(is_first, own, other, axis=0):
        first = jnp.where(is_first, own, other)
        second = jnp.where(is_first, other, own)
        return jnp.stack([first, second], axis=axis)

    def gather_micro(keep, got, core=None):
        count = keep.shape[0]
        cur = ordered(fs == 0, keep, got, axis=1)[:, :, None]
        for bit in range(bits):
            got = flip(cur, bit, core)
            cur = ordered((x >> bit) & 1 == 0, cur, got, axis=2).reshape(
                count, 2, 2 << bit, share, width
            )
        return cur.reshape(count, rows, width)

    def scatter_micro(streams):
        blocks = jnp.stack([v.reshape(2, share, width) for v in streams], axis=1)
        keep = lax.dynamic_index_in_dim(blocks, fs, 0, keepdims=False)
        give = lax.dynamic_index_in_dim(blocks, 1 - fs, 0, keepdims=False)
        return ordered(fs == 0, keep, flip(give, bits)).reshape(1, micro, share, width)

    class Reduction:
        def __init__(self, core, own, near):
            self.core, self.value, self.step = core, own, 0
            self.got = None if near is None else flip(near, bits, core)

        def forward(self, value):
            self.value = value
            inward, middle, outward = ((0, 1), (3, 2)), ((1, 2), (2, 1)), ((1, 0), (2, 3))
            self.got = z_on(self.value, self.core, (inward, middle, outward)[self.step])
            self.step += 1
            return self.value

    def z_sum(g, core):
        half = zs // 2
        for k in range(half - 1):
            got = z_on(g, core, [(k, k + 1), (zs - 1 - k, zs - 2 - k)])
            g = (g.astype(F32) + got.astype(F32)).astype(g.dtype)
        got = z_on(g, core, [(half - 1, half), (half, half - 1)])
        g = (g.astype(F32) + got.astype(F32)).astype(g.dtype)
        for k in reversed(range(half - 1)):
            got = z_on(g, core, [(k + 1, k), (zs - 2 - k, zs - 1 - k)])
            g = jnp.where((z == k) | (z == zs - 1 - k), got, g)
        return g

    streams = range(2)
    by_slot = layer_in[0].reshape(2, 2, share, width)
    src_keep = lax.dynamic_index_in_dim(by_slot, fs, 0, keepdims=False)
    src_give = lax.dynamic_index_in_dim(by_slot, 1 - fs, 0, keepdims=False)
    src_got = flip(src_give, bits)
    src = [gather_micro(src_keep[j : j + 1], src_got[j : j + 1])[0] for j in streams]
    segs = lax.dynamic_index_in_dim(
        segments.reshape(2, 2, 2, packed, length), fs, 1, keepdims=False
    )
    seg_e = [segs[0, j] for j in streams]
    seg_d = [segs[1, j] for j in streams]
    seg_own = [jnp.where(is0, e, d) for e, d in zip(seg_e, seg_d)]
    outer = (z == 0) | (z == zs - 1)
    flags = jnp.stack([sec, z % 2, outer]).astype(jnp.int32)

    def fetch(weights, core=None, deps=()):
        if len({w.shape[1] for w in weights}) > 1:
            return [fetch([w], core, deps)[0] for w in weights]
        p = flip(pack_rows(flags, weights, deps), bits, core)
        q = z_on(p, core, [(i, i ^ 1) for i in range(zs)])
        pairs, at = [], 0
        for w in weights:
            pairs.append((w, Near(w.shape, p, q, at)))
            at += w.shape[0] // 2
        return pairs

    STRICT[-1] = False
    (w_qkv,) = fetch([self_qkv[0]])
    (w_out,) = fetch([self_out[0]])
    early = [fetch([w[0]], 0, [src_got])[0] for w in (ffn_up, ffn_down)]
    (w_cross,) = fetch([cross_proj[0]], None, [src[1]])
    late = fetch([ffn_up[0], ffn_down[0]], 1, [src[1]])

    def row(v, i):
        return v[i : i + 1]

    def ln(i):
        return row(gain, i), row(bias, i)

    STRICT[-1] = True
    start, kept_in, sa, keep_s = ([None] * 2 for _ in range(4))
    for j in streams:
        start[j], *kept_in[j], qkv, o, lse, part = self_forward(
            flags, src[j], seg_own[j], *ln(1), w_qkv, w_out
        )
        keep_s[j] = (qkv, o, lse)
        sa[j] = tp_sum(part)
    mid, kept_e1, keep_fe, ff = ([None] * 2 for _ in range(4))
    for j in streams:
        mid[j], *kept_e1[j], hidden, slope, part = ffn_forward(
            0, flags, start[j], sa[j], *ln(0), *early
        )
        keep_fe[j] = (hidden, slope)
        ff[j] = tp_sum(part, 0)
    memory, kept_mem, kv, d1, kept_d1, q, ca, keep_c = ([None] * 2 for _ in range(8))
    for j in streams:
        d1[j], *kept_d1[j], q[j] = norm_project(1, flags, start[j], sa[j], *ln(0), w_cross)
        memory[j], *kept_mem[j], kv[j] = norm_project(0, flags, mid[j], ff[j], *ln(2), w_cross)
        kv[j] = to_core(kv[j], 1)
    cot_by_slot = cotangent.reshape(2, 2, share, width)
    cot_keep = lax.dynamic_index_in_dim(cot_by_slot, fs, 0, keepdims=False)
    cot_give = lax.dynamic_index_in_dim(cot_by_slot, 1 - fs, 0, keepdims=False)
    for j in streams:
        *keep_c[j], part = cross_forward(1, flags, q[j], kv[j], seg_d[j], seg_e[j], w_cross)
        ca[j] = tp_sum(part, 1)
    cot = gather_micro(cot_keep, flip(after(cot_give, keep_c[0][0]), bits, 1), 1)
    d2, kept_d2, keep_fd = ([None] * 2 for _ in range(3))
    for j in streams:
        d2[j], *kept_d2[j], hidden, slope, part = ffn_forward(
            1, flags, d1[j], ca[j], *ln(1), *late
        )
        keep_fd[j] = (hidden, slope)
        ff[j] = tp_sum(part, 1)

    STRICT[-1] = False
    def pick(items, i):
        return [item[i] for item in items]

    def height(group):
        return group[0][0].shape[1] // (2 if group[2] else 1)

    def reduced(enc, dec, cuts=1, sums=()):
        heights = {height(g) for g in (*enc, *dec)}
        widths = {sum(g[1][0].shape[1] // (1 if g[2] else 2) for g in own) for own in (enc, dec) if own}
        if len(heights) > 1 or len(widths) > 1:
            advance((sums, 0))
            return [reduced([g], [], cuts)[0] for g in enc] + [
                reduced([], [g], cuts)[0] for g in dec
            ]
        core = None if enc and dec else 0 if enc else 1
        blocks = weight_grads(flags, (enc, dec), (), cuts, sums)
        chains = [Reduction(core, *pair) for pair in zip(blocks[:cuts], blocks[cuts:])]
        places = []
        for own in (enc, dec):
            at = 0
            for lefts, rights, split_left in own:
                places.append((chains, at))
                at += rights[0].shape[1] // (1 if split_left else 2)
        return places

    def chains_of(places):
        return list({id(chain): chain for place in places for chain in place[0]}.values())

    def advance(*places, deps=()):
        chains = [chain for chain in chains_of(places) if chain.step < 3]
        if chains:
            pairs = [(chain.core, chain.value, chain.got) for chain in chains]
            for chain, value in zip(chains, add_pairs(flags, pairs, deps)):
                chain.forward(value)
        return chains

    def arrived(*places):
        return [chain.got for chain in chains_of(places)]

    def soon(pair):
        return (pair[0], after(pair[1]))

    decoded, df, du, back, n_out, n_d2, n_d1, n_mem, n_e1, n_in = ([None] * 2 for _ in range(10))
    for j in streams:
        decoded[j], df[j], n_out[j], du[j], part = top_backward(
            1, flags, d2[j], ff[j], cot[j], *ln(2), keep_fd[j][1], *late
        )
        back[j] = tp_sum(part, 1)

    dca, dq, dkv, dmem, ds, dqkv, grad_d, grad_e, dfe, due, backe = ([None] * 2 for _ in range(11))
    es, eqkv = ([None] * 2 for _ in range(2))

    def cross_step(j):
        dca[j], n_d2[j], dq[j], grad, part = cross_backward(
            1, flags, (df[j], *back[j]), kept_d2[j], row(gain, 1), q[j], kv[j], seg_d[j], seg_e[j],
            *keep_c[j], w_cross,
        )
        dkv[j] = to_core(grad, 0)
        dmem[j] = tp_sum(memory_backward(0, flags, dkv[j], w_cross), 0)
        back[j] = tp_sum(part, 1)

    def ffn_step(j):
        dfe[j], n_mem[j], due[j], part = ffn_backward(
            0, flags, dmem[j], kept_mem[j], row(gain, 2), keep_fe[j][1], *early,
        )
        backe[j] = tp_sum(part, 0)

    def dec_step(j, sums):
        ds[j], n_d1[j], dqkv[j], part = self_backward(
            1, flags, (dca[j], *back[j]), kept_d1[j], row(gain, 0), *keep_s[j], seg_own[j], w_qkv,
            w_out, sums=sums,
        )
        grad_d[j] = own_rows(ds[j]).astype(F32) + tp_scatter(part, 1)

    def enc_step(j):
        es[j], n_e1[j], eqkv[j], part = self_backward(
            0, flags, (dfe[j], *backe[j]), kept_e1[j], row(gain, 0), *keep_s[j], seg_own[j], w_qkv,
            w_out,
        )
        dy = own_rows(es[j]).astype(F32) + tp_scatter(part, 0)
        hat = own_rows(kept_in[j][0]).astype(F32)
        dv, n_in[j] = norm_back(dy, (hat, own_rows(kept_in[j][1])[:, :1]), gain[1])
        grad_e[j] = dv.astype(BF)

    cross_step(0)
    cross_step(1)
    (gd_down,) = reduced([], [(pick(keep_fd, 0), df, True)])
    ffn_step(0)
    (gd_up,) = reduced([], [(d2, du, False)])
    ffn_step(1)
    dec_step(0, gd_down[0])
    enc_step(0)
    dec_step(1, gd_down[0] + gd_up[0])
    ge_cross, ge_down, gd_cross, gd_qkv, gd_out = reduced(
        [(memory, dkv, False), (pick(keep_fe, 0), dfe, True)],
        [
            ((*d1, *dca), (*dq, *pick(keep_c, 0)), False),
            (start, dqkv, False),
            (ds, pick(keep_s, 1), False),
        ],
        2,
    )
    STRICT[-1] = True
    enc_step(1)
    advance(gd_up, gd_down)
    ge_up, ge_qkv, ge_out = reduced(
        [(mid, due, False), (start, eqkv, False), (es, pick(keep_s, 1), False)], [], 2
    )
    layer_out = scatter_micro([own_rows(jnp.where(is0, m, d)) for m, d in zip(memory, decoded)])

    def part(place, i):
        return ([place[0][i % len(place[0])]], 0)

    p1a, p1b = part(ge_cross, 0), part(ge_cross, 1)
    p2a, p2b = part(ge_up, 0), part(ge_up, 1)
    advance(p1a, gd_down, gd_up, deps=[layer_out])

    once = 1.0 / tp
    norms = jnp.where(
        is0,
        jnp.stack([sum(n_e1).sum(1) * once, sum(n_in), sum(n_mem).sum(1) * once], axis=1),
        jnp.stack([sum(n_d1), sum(n_d2), sum(n_out)], axis=1).sum(2) * once,
    )

    def total(enc, dec, columns, turned=False):
        kept, got = (
            [([getattr(chain, name) for chain in chains], at) for chains, at in (enc, dec)]
            for name in ("value", "got")
        )
        if columns % 128 == 0 and enc[1] % 128 == 0 and dec[1] % 128 == 0 and not turned:
            return finish(flags, kept, got, columns)[None]
        kept, got = (
            jnp.where(is0, *(jnp.concatenate(rows)[:, at : at + columns] for rows, at in pair))
            for pair in (kept, got)
        )
        kept = jnp.where(outer, got, kept)
        return (jnp.transpose(kept) if turned else kept).astype(F32)[None]

    def norms_step(norms, bit):
        bit_on = (t >> bit) & 1
        parts = norms.reshape(2, 3, 2, -1)
        return lax.dynamic_index_in_dim(parts, bit_on, 2, keepdims=False) + flip(
            lax.dynamic_index_in_dim(parts, 1 - bit_on, 2, keepdims=False), bit
        )

    hops = reversed(range(bits + 1))
    norms = norms_step(norms, next(hops))
    input_grad = scatter_micro([jnp.where(is0, e, d.astype(BF)) for e, d in zip(grad_e, grad_d)])
    advance(p1b, gd_up, p1a, deps=[*arrived(gd_down), norms])
    for bit in hops:
        norms = norms_step(norms, bit)
    norms_sum = Reduction(None, norms, None)
    advance(p2a, p1b, p1a, deps=[*arrived(gd_up), norms, input_grad])
    norms_sum.forward(norms)
    advance(p2b, p2a, p1b, deps=[*arrived(p1a), norms_sum.got])
    norms_sum.forward(norms_sum.value + norms_sum.got)
    advance(p2b, p2a, deps=[*arrived(p1b), norms_sum.got])
    norms_sum.forward(norms_sum.value + norms_sum.got)
    early_ends = all(chain.step == 3 for chain in chains_of([ge_cross, gd_cross, ge_down, gd_down]))
    if early_ends:
        g_cross = total(ge_cross, gd_cross, cross_proj.shape[2])
        g_down = total(ge_down, gd_down, width)
    advance(p2b, deps=[*arrived(p2a), norms_sum.got])
    everything = (
        ge_cross, ge_down, gd_cross, gd_qkv, gd_out, ge_up, ge_qkv, ge_out, gd_down, gd_up
    )
    while advance(*everything):
        pass
    if not early_ends:
        g_cross = total(ge_cross, gd_cross, cross_proj.shape[2])
        g_down = total(ge_down, gd_down, width)
    norms = jnp.where(outer, norms_sum.got, norms_sum.value)
    totals = (
        total(ge_qkv, gd_qkv, self_qkv.shape[2]),
        total(ge_out, gd_out, self_out.shape[1], True),
        g_cross, total(ge_up, gd_up, ffn_up.shape[2]), g_down,
    )
    return (layer_out, input_grad, *totals, norms[0][None], norms[1][None])


def solution(mesh):
    return jax.shard_map(
        on_device,
        mesh=mesh,
        in_specs=(
            P("section", None, ("dp", "tensor"), None),
            P(None, None, "dp", None),
            P(None, ("dp", "tensor"), None),
            P("section", None, "tensor"),
            P("section", "tensor", None),
            P("section", None, "tensor"),
            P("section", None, "tensor"),
            P("section", "tensor", None),
            P("section", None, None),
            P("section", None, None),
        ),
        out_specs=(
            P("section", None, ("dp", "tensor"), None),
            P("section", None, ("dp", "tensor"), None),
            P("section", None, "tensor"),
            P("section", "tensor", None),
            P("section", None, "tensor"),
            P("section", None, "tensor"),
            P("section", "tensor", None),
            P("section", None, "tensor"),
            P("section", None, "tensor"),
        ),
        check_vma=False,
    )
```
